128 devices in a mesh: branch: 16 (over y, x), tensor: 8 (over z, core).
Axes of the slice: x: 4, y: 4, z: 4, core: 2. Of those that a mesh axis runs over, the one named last changes fastest.
Arguments:
- queries: bfloat16 [4096, 8192], P('branch', 'tensor'), may hold values from -6 to 6
- keys: bfloat16 [4096, 1024], P('branch', 'tensor'), may hold values from -6 to 6
- values: bfloat16 [4096, 1024], P('branch', 'tensor'), may hold values from -6 to 6
- grad_out: bfloat16 [4096, 8192], P('branch', 'tensor'), may hold values from -6 to 6
- w_out: bfloat16 [8192, 8192], P('tensor'), may hold values from -0.0625 to 0.0625
- parent: int32 [16], replicated, may hold values from -1 to 14, as said below
Outputs:
- attn_out: bfloat16 [4096, 8192], P('branch', 'tensor')
- grad_queries: bfloat16 [4096, 8192], P('branch', 'tensor')
- grad_keys: bfloat16 [4096, 1024], P('branch', 'tensor')
- grad_values: bfloat16 [4096, 1024], P('branch', 'tensor')
The draws below stay inside these ranges and needn't reach their ends.
Inputs may be any that keep to these rules, and one draw needn't show every extreme that they name: parent of node 0 is -1; every other node's parent has a smaller index; the last node's parent is node 14.
All inputs are finite; a program needn't handle non-finite values.
Results may differ from the reference program's by a relative error of at most 0.04.
Values may be sent and summed in bfloat16 or wider, within the bound.
No kernel may reach another device: no remote copies, remote signals or barrier semaphores. Data moves between devices by JAX's collectives and lax.ppermute only.
A program may use at most 256 MiB of HBM per device.

```python
import math
import jax
import jax.numpy as jnp
from jax import lax

D = 8192
HEADS = 64
KV_HEADS = 8
HEAD_DIM = 128
SEG = 256
NODES = 16
TOKENS = 4096


def draw_queries(key, part):
    key = jax.random.fold_in(key, 11)
    entries = jnp.clip(jax.random.normal(key, (TOKENS, HEADS * HEAD_DIM), jnp.float32), -6.0, 6.0)
    return entries.astype(jnp.bfloat16)


def draw_keys(key, part):
    key = jax.random.fold_in(key, 13)
    entries = jnp.clip(jax.random.normal(key, (TOKENS, KV_HEADS * HEAD_DIM), jnp.float32), -6.0, 6.0)
    return entries.astype(jnp.bfloat16)


def draw_parent(key, part):
    key = jax.random.fold_in(key, 17)
    node_ids = jnp.arange(NODES, dtype=jnp.int32)
    upper = jnp.maximum(node_ids, 1)
    chosen = jax.random.randint(key, (NODES,), 0, upper, dtype=jnp.int32)
    chosen = jnp.where(node_ids == NODES - 1, NODES - 2, chosen)
    return jnp.where(node_ids == 0, -1, chosen).astype(jnp.int32)


def shard_levels(rng, dims, pieces, smallest, high):
    level, own = 1.0, jax.random.fold_in(rng, 6)
    for axis_at, blocks in pieces:
        draws = jnp.exp(jax.random.uniform(jax.random.fold_in(own, axis_at), (blocks,), jnp.float32, smallest / len(pieces), high / len(pieces)))
        level = level * jnp.repeat(draws, dims[axis_at] // blocks).reshape([-1 if axis == axis_at else 1 for axis in range(len(dims))])
    return level


def noise(stream_key, extent, deviation, reach, shards=(), kind=jnp.bfloat16):
    gain = shard_levels(stream_key, extent, shards, -0.22, 0.18) if shards else 1.0
    result = jax.random.normal(stream_key, extent, jnp.float32) * deviation * gain
    return jnp.minimum(jnp.maximum(result, -reach), reach).astype(kind)


def setup_inputs(seed: int = 0) -> dict:
    key_of = jax.random.split(jax.random.key(seed), 7)
    queries = draw_queries(jax.random.fold_in(key_of[6], 71), 0)
    keys = draw_keys(jax.random.fold_in(key_of[6], 71), 0)
    values = noise(key_of[2], (TOKENS, KV_HEADS * HEAD_DIM), 1.0, 6.0, ((0, 16), (1, 8)))
    grad_out = noise(key_of[3], (TOKENS, D), 1.0, 6.0, ((0, 16), (1, 8)))
    w_out = noise(key_of[4], (HEADS * HEAD_DIM, D), (HEADS * HEAD_DIM) ** -0.5, 0.0625, ((0, 8),))
    parent = draw_parent(jax.random.fold_in(key_of[6], 71), 0)
    return dict(queries=queries, keys=keys, values=values, grad_out=grad_out, w_out=w_out, parent=parent)


def ancestor_table(parent, node_count):
    indices = jnp.arange(node_count, dtype=jnp.int32)

    def climb_up(state_now, unused):
        current, marked = state_now
        onehot = current[:, None] == indices[None, :]
        marked = jnp.logical_or(marked, onehot)
        upward = lax.optimization_barrier(jnp.sum(jnp.where(onehot, parent[None, :], 0), axis=1)).astype(jnp.int32)
        upward = jnp.where(current >= 0, upward, -1).astype(jnp.int32)
        return ((upward, marked), None)
    start_state = (parent.astype(jnp.int32), jnp.zeros((node_count, node_count), dtype=jnp.bool_))
    (unused_last, marked), unused_out = lax.scan(climb_up, start_state, None, length=node_count)
    return marked

def reference(queries, keys, values, grad_out, w_out, parent):
    group_size = HEADS // KV_HEADS
    score_scale = 1.0 / math.sqrt(HEAD_DIM)
    marked = ancestor_table(parent, NODES)
    token_ids = jnp.arange(TOKENS, dtype=jnp.int32)
    token_node = token_ids // SEG
    token_pos = token_ids % SEG
    visible = marked[token_node][:, token_node]
    same_node = token_node[:, None] == token_node[None, :]
    visible = jnp.logical_or(visible, jnp.logical_and(same_node, token_pos[None, :] <= token_pos[:, None]))
    head_grads = jnp.dot(grad_out, w_out.T, preferred_element_type=jnp.float32).astype(jnp.bfloat16)
    query_heads = queries.reshape(TOKENS, KV_HEADS, group_size, HEAD_DIM).transpose(1, 2, 0, 3)
    grad_heads = head_grads.reshape(TOKENS, KV_HEADS, group_size, HEAD_DIM).transpose(1, 2, 0, 3)
    key_heads = keys.reshape(TOKENS, KV_HEADS, HEAD_DIM).transpose(1, 0, 2)
    value_heads = values.reshape(TOKENS, KV_HEADS, HEAD_DIM).transpose(1, 0, 2)

    def one_group(operands):
        query_group, grad_group, key_one, value_one = operands
        outputs = []
        query_grads = []
        key_grad = jnp.zeros((TOKENS, HEAD_DIM), jnp.float32)
        value_grad = jnp.zeros((TOKENS, HEAD_DIM), jnp.float32)
        for member in range(group_size):
            query_one = query_group[member]
            grad_one = grad_group[member]
            scores = jnp.dot(query_one, key_one.T, preferred_element_type=jnp.float32) * score_scale
            masked = jnp.where(visible, scores, -jnp.inf)
            row_max = lax.optimization_barrier(jnp.max(masked, axis=1))
            log_total = row_max + jnp.log(lax.optimization_barrier(jnp.sum(jnp.exp(masked - row_max[:, None]), axis=1)))
            attention = jnp.exp(masked - log_total[:, None])
            attention_b = attention.astype(jnp.bfloat16)
            attended = jnp.dot(attention_b, value_one, preferred_element_type=jnp.float32).astype(jnp.bfloat16)
            row_delta = lax.optimization_barrier(jnp.sum(grad_one.astype(jnp.float32) * attended.astype(jnp.float32), axis=1))
            dprobs = jnp.dot(grad_one, value_one.T, preferred_element_type=jnp.float32)
            dscores = (attention * (dprobs - row_delta[:, None])).astype(jnp.bfloat16)
            query_grads.append(jnp.dot(dscores, key_one, preferred_element_type=jnp.float32) * score_scale)
            key_grad = key_grad + jnp.dot(dscores.T, query_one, preferred_element_type=jnp.float32) * score_scale
            value_grad = value_grad + jnp.dot(attention_b.T, grad_one, preferred_element_type=jnp.float32)
            outputs.append(attended)
        return (jnp.stack(outputs), jnp.stack(query_grads), key_grad, value_grad)
    attended, query_grad, key_grad, value_grad = lax.map(one_group, (query_heads, grad_heads, key_heads, value_heads))
    attn_out = attended.transpose(2, 0, 1, 3).reshape(TOKENS, HEADS * HEAD_DIM)
    grad_queries = query_grad.transpose(2, 0, 1, 3).reshape(TOKENS, HEADS * HEAD_DIM).astype(jnp.bfloat16)
    grad_keys = key_grad.transpose(1, 0, 2).reshape(TOKENS, KV_HEADS * HEAD_DIM).astype(jnp.bfloat16)
    grad_values = value_grad.transpose(1, 0, 2).reshape(TOKENS, KV_HEADS * HEAD_DIM).astype(jnp.bfloat16)
    return (attn_out, grad_queries, grad_keys, grad_values)
```

```python
import math

import jax
import jax.numpy as jnp
from jax import lax
from jax.experimental import pallas as pl
from jax.experimental.pallas import tpu as pltpu
from jax.sharding import PartitionSpec as P

HEAD_DIM = 128
SEG = 256
NODES = 16
GROUP = 8
SCALE = 1.0 / math.sqrt(HEAD_DIM)
EXP2_SCALE = SCALE * math.log2(math.e)
NEG_FLOOR = -1e30
VMEM_LIMIT = 48 * 1024 * 1024

NT = (((1,), (1,)), ((), ()))
NN = (((1,), (0,)), ((), ()))


def matmul(left, right, dims=NN):
    return lax.dot_general(left, right, dims, preferred_element_type=jnp.float32)


def list_visible(parent_ref, own, visible_ref):
    visible_ref[0] = own

    def climb(state):
        node, count = state
        above = parent_ref[node]
        visible_ref[count] = above
        return above, count + 1

    def has_parent(state):
        node, count = state
        return jnp.logical_and(parent_ref[node] >= 0, count < NODES)

    return lax.while_loop(has_parent, climb, (own, jnp.int32(1)))[1]


def forward_kernel(
    parent_ref, q_ref, kv_ref, out_ref, factor_ref, weights_hbm,
    visible_ref, kv_buf, weights_buf, acc_ref, max_ref, sum_ref, seen_max_ref, kv_sem, weights_sem,
):
    own = lax.axis_index("branch")
    count = list_visible(parent_ref, own, visible_ref)

    def kv_copy(i):
        return pltpu.make_async_copy(kv_ref.at[visible_ref[i]], kv_buf.at[i], kv_sem.at[i])

    def weights_copy(i):
        return pltpu.make_async_copy(weights_buf.at[i], weights_hbm.at[i], weights_sem.at[i])

    def start_kv(i, unused):
        kv_copy(i).start()
        return unused

    lax.fori_loop(0, count, start_kv, 0)

    def block(i, is_own):
        kv_copy(i).wait()
        keys = kv_buf[i, :, :HEAD_DIM]
        values_t = kv_buf[i, :, HEAD_DIM:].astype(jnp.float32).T.astype(jnp.bfloat16)
        for h in range(GROUP):
            rows = pl.ds(h * SEG, SEG)
            scores = matmul(keys, q_ref[:, h * HEAD_DIM : (h + 1) * HEAD_DIM], NT)
            if is_own:
                key_pos = lax.broadcasted_iota(jnp.int32, (SEG, SEG), 0)
                row_pos = lax.broadcasted_iota(jnp.int32, (SEG, SEG), 1)
                scores = jnp.where(key_pos <= row_pos, scores, NEG_FLOOR)
            block_max = jnp.max(scores, axis=0, keepdims=True)
            if is_own:
                new_max = block_max
            else:
                old_max = max_ref[h : h + 1, :]
                new_max = jnp.maximum(old_max, block_max)
            weights = jnp.exp2((scores - new_max) * EXP2_SCALE)
            block_sum = jnp.sum(weights, axis=0, keepdims=True)
            weights_b = weights.astype(jnp.bfloat16)
            weights_buf[i, :, rows] = weights_b
            part = matmul(values_t, weights_b)
            if is_own:
                acc_ref[h] = part
                sum_ref[h : h + 1, :] = block_sum
            else:
                shrink = jnp.exp2((old_max - new_max) * EXP2_SCALE)
                acc_ref[h] = acc_ref[h] * shrink + part
                sum_ref[h : h + 1, :] = sum_ref[h : h + 1, :] * shrink + block_sum
            max_ref[h : h + 1, :] = new_max
        seen_max_ref[i] = max_ref[...]
        weights_copy(i).start()

    block(0, True)

    def ancestor(i, unused):
        block(i, False)
        return unused

    lax.fori_loop(1, count, ancestor, 0)
    inverse = 1.0 / sum_ref[...]
    final_max = max_ref[...]

    def finish(i, unused):
        factor_ref[i] = jnp.exp2((seen_max_ref[i] - final_max) * EXP2_SCALE) * inverse
        return unused

    lax.fori_loop(0, count, finish, 0)
    for h in range(GROUP):
        out = acc_ref[h] * inverse[h : h + 1, :]
        out_ref[:, h * HEAD_DIM : (h + 1) * HEAD_DIM] = out.T.astype(jnp.bfloat16)

    def drain(i, unused):
        weights_copy(i).wait()
        return unused

    lax.fori_loop(0, count, drain, 0)


def forward(parent, queries, kv_all):
    return pl.pallas_call(
        forward_kernel,
        out_shape=(
            jax.ShapeDtypeStruct((SEG, GROUP * HEAD_DIM), jnp.bfloat16),
            jax.ShapeDtypeStruct((NODES, GROUP, SEG), jnp.float32),
            jax.ShapeDtypeStruct((NODES, SEG, GROUP * SEG), jnp.bfloat16),
        ),
        in_specs=[
            pl.BlockSpec(memory_space=pltpu.SMEM),
            pl.BlockSpec(memory_space=pltpu.VMEM),
            pl.BlockSpec(memory_space=pl.ANY),
        ],
        out_specs=(
            pl.BlockSpec(memory_space=pltpu.VMEM),
            pl.BlockSpec(memory_space=pltpu.VMEM),
            pl.BlockSpec(memory_space=pl.ANY),
        ),
        scratch_shapes=[
            pltpu.SMEM((NODES,), jnp.int32),
            pltpu.VMEM((NODES, SEG, 2 * HEAD_DIM), jnp.bfloat16),
            pltpu.VMEM((NODES, SEG, GROUP * SEG), jnp.bfloat16),
            pltpu.VMEM((GROUP, HEAD_DIM, SEG), jnp.float32),
            pltpu.VMEM((GROUP, SEG), jnp.float32),
            pltpu.VMEM((GROUP, SEG), jnp.float32),
            pltpu.VMEM((NODES, GROUP, SEG), jnp.float32),
            pltpu.SemaphoreType.DMA((NODES,)),
            pltpu.SemaphoreType.DMA((NODES,)),
        ],
        compiler_params=pltpu.CompilerParams(vmem_limit_bytes=VMEM_LIMIT),
        cost_estimate=pl.CostEstimate(flops=2 * 10**9, bytes_accessed=8 * 2**20, transcendentals=3 * 10**6),
        name="attend",
    )(parent, queries, kv_all)


def backward_kernel(
    parent_ref, q_ref, grad_ref, out_ref, factor_ref, kv_ref, weights_hbm, dq_ref, dkv_ref,
    visible_ref, kv_buf, weights_buf, dq_acc, delta_ref, kv_sem, weights_sem,
):
    own = lax.axis_index("branch")
    count = list_visible(parent_ref, own, visible_ref)

    def kv_copy(i):
        return pltpu.make_async_copy(kv_ref.at[visible_ref[i]], kv_buf.at[i], kv_sem.at[i])

    def weights_copy(i):
        return pltpu.make_async_copy(weights_hbm.at[i], weights_buf.at[i], weights_sem.at[i])

    def start(i, unused):
        kv_copy(i).start()
        weights_copy(i).start()
        return unused

    lax.fori_loop(0, count, start, 0)
    dkv_ref[...] = jnp.zeros_like(dkv_ref)
    dq_acc[...] = jnp.zeros_like(dq_acc)
    for h in range(GROUP):
        cols = slice(h * HEAD_DIM, (h + 1) * HEAD_DIM)
        products = grad_ref[:, cols].astype(jnp.float32) * out_ref[:, cols].astype(jnp.float32)
        sums = lax.dot_general(
            jnp.ones((GROUP, HEAD_DIM), jnp.float32), products, NT,
            precision=lax.Precision.HIGHEST, preferred_element_type=jnp.float32,
        )
        delta_ref[h : h + 1, :] = sums[0:1, :]

    def block(i, unused):
        kv_copy(i).wait()
        weights_copy(i).wait()
        keys = kv_buf[i, :, :HEAD_DIM]
        values = kv_buf[i, :, HEAD_DIM:]
        keys_t = keys.astype(jnp.float32).T.astype(jnp.bfloat16)
        key_grad = jnp.zeros((SEG, HEAD_DIM), jnp.float32)
        value_grad = jnp.zeros((SEG, HEAD_DIM), jnp.float32)
        for h in range(GROUP):
            cols = slice(h * HEAD_DIM, (h + 1) * HEAD_DIM)
            probs = weights_buf[i, :, pl.ds(h * SEG, SEG)].astype(jnp.float32) * factor_ref[i, h : h + 1, :]
            dprobs = matmul(values, grad_ref[:, cols], NT)
            dscores = (probs * (dprobs - delta_ref[h : h + 1, :])).astype(jnp.bfloat16)
            value_grad = value_grad + matmul(probs.astype(jnp.bfloat16), grad_ref[:, cols])
            key_grad = key_grad + matmul(dscores, q_ref[:, cols])
            dq_acc[h] += matmul(keys_t, dscores)
        node = visible_ref[i]
        dkv_ref[node, :, :HEAD_DIM] = (key_grad * SCALE).astype(jnp.bfloat16)
        dkv_ref[node, :, HEAD_DIM:] = value_grad.astype(jnp.bfloat16)
        return unused

    lax.fori_loop(0, count, block, 0)
    for h in range(GROUP):
        dq_ref[:, h * HEAD_DIM : (h + 1) * HEAD_DIM] = (dq_acc[h] * SCALE).T.astype(jnp.bfloat16)


def backward(parent, queries, head_grads, attn_out, factors, kv_all, weights):
    vmem = pl.BlockSpec(memory_space=pltpu.VMEM)
    hbm = pl.BlockSpec(memory_space=pl.ANY)
    return pl.pallas_call(
        backward_kernel,
        out_shape=(
            jax.ShapeDtypeStruct((SEG, GROUP * HEAD_DIM), jnp.bfloat16),
            jax.ShapeDtypeStruct((NODES, SEG, 2 * HEAD_DIM), jnp.bfloat16),
        ),
        in_specs=[pl.BlockSpec(memory_space=pltpu.SMEM), vmem, vmem, vmem, vmem, hbm, hbm],
        out_specs=(vmem, vmem),
        scratch_shapes=[
            pltpu.SMEM((NODES,), jnp.int32),
            pltpu.VMEM((NODES, SEG, 2 * HEAD_DIM), jnp.bfloat16),
            pltpu.VMEM((NODES, SEG, GROUP * SEG), jnp.bfloat16),
            pltpu.VMEM((GROUP, HEAD_DIM, SEG), jnp.float32),
            pltpu.VMEM((GROUP, SEG), jnp.float32),
            pltpu.SemaphoreType.DMA((NODES,)),
            pltpu.SemaphoreType.DMA((NODES,)),
        ],
        compiler_params=pltpu.CompilerParams(vmem_limit_bytes=VMEM_LIMIT),
        cost_estimate=pl.CostEstimate(flops=4 * 10**9, bytes_accessed=8 * 2**20, transcendentals=0),
        name="attend_grads",
    )(parent, queries, head_grads, attn_out, factors, kv_all, weights)


def per_device(queries, keys, values, grad_out, w_out, parent):
    kv = jnp.concatenate([keys, values], axis=1)
    kv_all = lax.all_gather(kv, "branch", axis=0)
    grad_all = lax.all_gather(grad_out, "tensor", axis=1, tiled=True)
    attn_out, factors, weights = forward(parent, queries, kv_all)
    head_grads = jnp.einsum(
        "rn,hn->rh", grad_all, w_out, preferred_element_type=jnp.float32
    ).astype(jnp.bfloat16)
    grad_queries, dkv = backward(parent, queries, head_grads, attn_out, factors, kv_all, weights)
    own = lax.psum_scatter(
        dkv.reshape(NODES * SEG, 2 * HEAD_DIM), "branch", scatter_dimension=0, tiled=True
    )
    return attn_out, grad_queries, own[:, :HEAD_DIM], own[:, HEAD_DIM:]


def solution(mesh):
    return jax.shard_map(
        per_device,
        mesh=mesh,
        in_specs=(
            P("branch", "tensor"),
            P("branch", "tensor"),
            P("branch", "tensor"),
            P("branch", "tensor"),
            P("tensor", None),
            P(),
        ),
        out_specs=(P("branch", "tensor"),) * 4,
        check_vma=False,
    )
```

```python
import functools
import math

import jax
import jax.numpy as jnp
from jax import lax
from jax.experimental import pallas as pl
from jax.experimental.pallas import tpu as pltpu
from jax.sharding import PartitionSpec as P

HEAD_DIM = 128
SEG = 256
NODES = 16
SIDE = 4
GROUP = 8
SCALE = 1.0 / math.sqrt(HEAD_DIM)
EXP2_SCALE = SCALE * math.log2(math.e)
NEG_FLOOR = -1e30
VMEM_LIMIT = 60 * 1024 * 1024
DEEP = 2 * HEAD_DIM
TILE = 16
SUM_LIMIT = 2.0**30

NT = (((1,), (1,)), ((), ()))
NN = (((1,), (0,)), ((), ()))


def matmul(left, right, dims=NN):
    return lax.dot_general(left, right, dims, preferred_element_type=jnp.float32)


def list_visible(parent_ref, own, visible_ref):
    visible_ref[0] = own

    def climb(state):
        node, count = state
        above = parent_ref[node]
        visible_ref[count] = above
        return above, count + 1

    def has_parent(state):
        node, count = state
        return jnp.logical_and(parent_ref[node] >= 0, count < NODES)

    return lax.while_loop(has_parent, climb, (own, jnp.int32(1)))[1]


def ring(count, shift):
    return [(i, (i + shift) % count) for i in range(count)]


def along_x(shift):
    return [(y * SIDE + x, y * SIDE + (x + shift) % SIDE) for y in range(SIDE) for x in range(SIDE)]


def along_y(shift):
    return [(y * SIDE + x, ((y + shift) % SIDE) * SIDE + x) for y in range(SIDE) for x in range(SIDE)]


def offsets(own, node):
    behind_y = lax.rem(lax.div(own, SIDE) - lax.div(node, SIDE) + SIDE, SIDE)
    behind_x = lax.rem(lax.rem(own, SIDE) - lax.rem(node, SIDE) + SIDE, SIDE)
    return behind_y, behind_x


def start_kv(i, own, visible_ref, key_refs, value_refs, key_buf, value_buf, kv_sem):
    node = visible_ref[i]
    behind_y, behind_x = offsets(own, node)
    for step in range(SIDE):

        @pl.when(behind_y == step)
        def _():
            source = key_refs[step].at[behind_x]
            pltpu.make_async_copy(source, key_buf.at[i, :, pl.ds(0, HEAD_DIM)], kv_sem.at[0, i]).start()

        @pl.when(behind_x == step)
        def _():
            source = value_refs[step].at[behind_y]
            pltpu.make_async_copy(source, value_buf.at[i, :, pl.ds(0, HEAD_DIM)], kv_sem.at[1, i]).start()


def wait_kv(i, key_refs, value_refs, key_buf, value_buf, kv_sem):
    lanes = pl.ds(0, HEAD_DIM)
    pltpu.make_async_copy(key_refs[0].at[0], key_buf.at[i, :, lanes], kv_sem.at[0, i]).wait()
    pltpu.make_async_copy(value_refs[0].at[0], value_buf.at[i, :, lanes], kv_sem.at[1, i]).wait()


def repeat(first, last, do):
    def step(i, unused):
        do(i)
        return unused

    lax.fori_loop(first, last, step, 0)


def head(h):
    return slice(h * HEAD_DIM, (h + 1) * HEAD_DIM)


def head_rows(h):
    return slice(h * SEG, (h + 1) * SEG)


def unit_lanes(count):
    lane = lax.broadcasted_iota(jnp.int32, (SEG, HEAD_DIM), 1)
    return jnp.where(lane < count, 1.0, 0.0).astype(jnp.bfloat16)


def top_rows(rows):
    place = lax.broadcasted_iota(jnp.int32, (TILE, SEG), 0)
    tile = jnp.zeros((TILE, SEG), jnp.float32)
    for n, row in enumerate(rows):
        tile = jnp.where(place == n, row, tile)
    return tile.astype(jnp.bfloat16)


def rounded(values):
    return values.astype(jnp.bfloat16).astype(jnp.float32)


def forward_kernel(
    parent_ref, q_hbm, k0, k1, k2, k3, v0, v1, v2, v3, out_hbm, out_t_hbm, inverse_ref, weights_hbm,
    visible_ref, q_ref, q_deep_ref, out_ref, out_t_ref, key_buf, value_buf, values_t_ref, weights_buf,
    score_ref, acc_ref, max_ref, kv_sem, weights_sem, one_sem,
):
    key_refs, value_refs = (k0, k1, k2, k3), (v0, v1, v2, v3)
    own = lax.axis_index("branch")
    q_copy = pltpu.make_async_copy(q_hbm, q_ref, one_sem.at[0])
    q_copy.start()
    count = list_visible(parent_ref, own, visible_ref)
    repeat(0, count, lambda i: start_kv(i, own, visible_ref, key_refs, value_refs, key_buf, value_buf, kv_sem))

    def fill(i):
        key_buf[i, :, HEAD_DIM:] = unit_lanes(1)

    repeat(0, count, fill)
    values_t_ref[HEAD_DIM:, :] = jnp.ones((TILE, SEG), jnp.bfloat16)
    q_deep_ref[:, HEAD_DIM:, :] = jnp.zeros((GROUP, HEAD_DIM, SEG), jnp.bfloat16)
    q_copy.wait()
    for h in range(GROUP):
        q_deep_ref[h, :HEAD_DIM, :] = q_ref[:, head(h)].T

    def weights_copy(i):
        return pltpu.make_async_copy(weights_buf.at[i], weights_hbm.at[i], weights_sem.at[i])

    def set_shift(h, row):
        q_deep_ref[h, HEAD_DIM : HEAD_DIM + TILE, :] = top_rows([-row])

    def own_scores(h):
        key_pos = lax.broadcasted_iota(jnp.int32, (SEG, SEG), 0)
        row_pos = lax.broadcasted_iota(jnp.int32, (SEG, SEG), 1)
        return jnp.where(key_pos <= row_pos, matmul(key_buf[0], q_deep_ref[h]), NEG_FLOOR)

    def values_in(i):
        values_t_ref[:HEAD_DIM, :] = value_buf[i, :, :HEAD_DIM].T

    def block(i):
        values_in(i)
        for h in range(GROUP):
            weights = jnp.exp2(matmul(key_buf[i], q_deep_ref[h]) * EXP2_SCALE)
            weights_buf[i, :, head_rows(h)] = weights.astype(jnp.bfloat16)
        for h in range(GROUP):
            acc_ref[h] += matmul(values_t_ref[...], weights_buf[i, :, head_rows(h)])
        weights_copy(i).start()

    def own_block(scores_of):
        values_in(0)
        for h in range(GROUP):
            weights = jnp.exp2(scores_of(h) * EXP2_SCALE)
            weights_buf[0, :, head_rows(h)] = weights.astype(jnp.bfloat16)
        for h in range(GROUP):
            acc_ref[h] = matmul(values_t_ref[...], weights_buf[0, :, head_rows(h)])
        weights_copy(0).start()

    wait_kv(0, key_refs, value_refs, key_buf, value_buf, kv_sem)
    for h in range(GROUP):
        scores = own_scores(h)
        score_ref[h] = scores
        max_ref[h : h + 1, :] = rounded(jnp.max(scores, axis=0, keepdims=True))
    for h in range(GROUP):
        set_shift(h, max_ref[h : h + 1, :])
    own_block(lambda h: score_ref[h] - max_ref[h : h + 1, :])

    def first_visit(i):
        wait_kv(i, key_refs, value_refs, key_buf, value_buf, kv_sem)
        block(i)

    repeat(1, count, first_visit)
    sums = acc_ref[:, HEAD_DIM, :]
    too_large = jnp.max(jnp.where(sums < SUM_LIMIT, 0.0, 1.0)) > 0.0

    @pl.when(too_large)
    def _():
        repeat(0, count, lambda i: weights_copy(i).wait())
        for h in range(GROUP):
            set_shift(h, jnp.zeros((1, SEG), jnp.float32))

        def raise_max(i):
            for h in range(GROUP):
                block_max = jnp.max(matmul(key_buf[i], q_deep_ref[h]), axis=0, keepdims=True)
                max_ref[h : h + 1, :] = jnp.maximum(max_ref[h : h + 1, :], block_max)

        repeat(1, count, raise_max)
        for h in range(GROUP):
            set_shift(h, rounded(max_ref[h : h + 1, :]))
        own_block(own_scores)
        repeat(1, count, block)

    inverse = 1.0 / acc_ref[:, HEAD_DIM, :]
    inverse_ref[...] = inverse
    for h in range(GROUP):
        out = acc_ref[h, :HEAD_DIM, :] * inverse[h : h + 1, :]
        out_t_ref[head(h), :] = out.astype(jnp.bfloat16)
        out_ref[:, head(h)] = out.T.astype(jnp.bfloat16)
    copies = [
        pltpu.make_async_copy(out_ref, out_hbm, one_sem.at[1]),
        pltpu.make_async_copy(out_t_ref, out_t_hbm, one_sem.at[2]),
    ]
    for copy in copies:
        copy.start()
    repeat(0, count, lambda i: weights_copy(i).wait())
    for copy in copies:
        copy.wait()


SMEM_SPEC = pl.BlockSpec(memory_space=pltpu.SMEM)
VMEM_SPEC = pl.BlockSpec(memory_space=pltpu.VMEM)
HBM_SPEC = pl.BlockSpec(memory_space=pl.ANY)
WIDTH = GROUP * HEAD_DIM


def bf16(*shape):
    return jax.ShapeDtypeStruct(shape, jnp.bfloat16)


def vmem16(*shape):
    return pltpu.VMEM(shape, jnp.bfloat16)


def vmem32(*shape):
    return pltpu.VMEM(shape, jnp.float32)


def forward(parent, queries, key_rows, value_rows):
    return pl.pallas_call(
        forward_kernel,
        out_shape=(
            bf16(SEG, WIDTH),
            bf16(WIDTH, SEG),
            jax.ShapeDtypeStruct((GROUP, SEG), jnp.float32),
            bf16(NODES, SEG, GROUP * SEG),
        ),
        in_specs=[SMEM_SPEC] + [HBM_SPEC] * 9,
        out_specs=(HBM_SPEC, HBM_SPEC, VMEM_SPEC, HBM_SPEC),
        scratch_shapes=[
            pltpu.SMEM((NODES,), jnp.int32),
            vmem16(SEG, WIDTH),
            vmem16(GROUP, DEEP, SEG),
            vmem16(SEG, WIDTH),
            vmem16(WIDTH, SEG),
            vmem16(NODES, SEG, DEEP),
            vmem16(NODES, SEG, DEEP),
            vmem16(HEAD_DIM + TILE, SEG),
            vmem16(NODES, SEG, GROUP * SEG),
            vmem32(GROUP, SEG, SEG),
            vmem32(GROUP, HEAD_DIM + TILE, SEG),
            vmem32(GROUP, SEG),
            pltpu.SemaphoreType.DMA((2, NODES)),
            pltpu.SemaphoreType.DMA((NODES,)),
            pltpu.SemaphoreType.DMA((3,)),
        ],
        compiler_params=pltpu.CompilerParams(vmem_limit_bytes=VMEM_LIMIT),
        cost_estimate=pl.CostEstimate(flops=2 * 10**9, bytes_accessed=8 * 2**20, transcendentals=3 * 10**6),
        name="attend",
    )(parent, queries, *key_rows, *value_rows)


def backward_kernel(
    parent_ref, q_hbm, grad_t_hbm, out_t_hbm, inverse_ref, k0, k1, k2, k3, v0, v1, v2, v3, weights_hbm,
    dq_hbm, dk0, dk1, dk2, dk3, dv0, dv1, dv2, dv3,
    visible_ref, q_ref, grad_t_ref, out_t_ref, q_tall_ref, grad_tall_ref, grad_deep_ref, dq_ref,
    key_buf, value_buf, weights_buf, dscore_ref, dk_ref, dv_ref, dq_acc, kv_sem, weights_sem, one_sem,
):
    key_refs, value_refs = (k0, k1, k2, k3), (v0, v1, v2, v3)
    own = lax.axis_index("branch")
    loads = [
        pltpu.make_async_copy(source, target, one_sem.at[n])
        for n, (source, target) in enumerate(((grad_t_hbm, grad_t_ref), (out_t_hbm, out_t_ref), (q_hbm, q_ref)))
    ]
    for load in loads:
        load.start()
    count = list_visible(parent_ref, own, visible_ref)

    def weights_copy(i):
        return pltpu.make_async_copy(weights_hbm.at[i], weights_buf.at[i], weights_sem.at[i])

    def start(i):
        start_kv(i, own, visible_ref, key_refs, value_refs, key_buf, value_buf, kv_sem)
        weights_copy(i).start()

    repeat(0, count, start)

    def fill(i):
        value_buf[i, :, HEAD_DIM:] = unit_lanes(3)

    repeat(0, count, fill)
    dk_ref[...] = jnp.zeros_like(dk_ref)
    dv_ref[...] = jnp.zeros_like(dv_ref)
    dq_acc[...] = jnp.zeros_like(dq_acc)
    grad_deep_ref[:, HEAD_DIM:, :] = jnp.zeros((GROUP, HEAD_DIM, SEG), jnp.bfloat16)
    for load in loads:
        load.wait()
    for h in range(GROUP):
        grad_t = (grad_t_ref[head(h), :].astype(jnp.float32) * inverse_ref[h : h + 1, :]).astype(jnp.bfloat16)
        grad_deep_ref[h, :HEAD_DIM, :] = grad_t
        grad_tall_ref[head_rows(h), :] = grad_t.T
        q_tall_ref[head_rows(h), :] = q_ref[:, head(h)]
        products = grad_t.astype(jnp.float32) * out_t_ref[head(h), :].astype(jnp.float32)
        delta = -jnp.sum(products, axis=0, keepdims=True)
        high = rounded(delta)
        middle = rounded(delta - high)
        grad_deep_ref[h, HEAD_DIM : HEAD_DIM + TILE, :] = top_rows([high, middle, delta - high - middle])

    def block(i):
        wait_kv(i, key_refs, value_refs, key_buf, value_buf, kv_sem)
        weights_copy(i).wait()
        keys_t = key_buf[i, :, :HEAD_DIM].T
        for h in range(GROUP):
            lowered = matmul(value_buf[i], grad_deep_ref[h])
            weights = weights_buf[i, :, head_rows(h)].astype(jnp.float32)
            dscore_ref[:, head_rows(h)] = (weights * lowered).astype(jnp.bfloat16)
        behind_y, behind_x = offsets(own, visible_ref[i])
        value_grad = matmul(weights_buf[i], grad_tall_ref[...])
        dv_ref[behind_x, behind_y] = value_grad.astype(jnp.bfloat16)
        key_grad = matmul(dscore_ref[...], q_tall_ref[...])
        dk_ref[behind_y, behind_x] = (key_grad * SCALE).astype(jnp.bfloat16)
        dq_acc[...] += matmul(keys_t, dscore_ref[...])

    repeat(0, count, block)
    stores = [
        pltpu.make_async_copy(dk_ref.at[n], target, kv_sem.at[0, n]) for n, target in enumerate((dk0, dk1, dk2, dk3))
    ] + [
        pltpu.make_async_copy(dv_ref.at[n], target, kv_sem.at[1, n]) for n, target in enumerate((dv0, dv1, dv2, dv3))
    ]
    for store in stores:
        store.start()
    for h in range(GROUP):
        dq_ref[:, head(h)] = (dq_acc[:, head_rows(h)] * SCALE).T.astype(jnp.bfloat16)
    dq_copy = pltpu.make_async_copy(dq_ref, dq_hbm, one_sem.at[0])
    dq_copy.start()
    for store in stores:
        store.wait()
    dq_copy.wait()


def backward(parent, queries, grad_t, out_t, inverse, key_rows, value_rows, weights):
    return pl.pallas_call(
        backward_kernel,
        out_shape=(bf16(SEG, WIDTH),) + (bf16(SIDE, SEG, HEAD_DIM),) * 8,
        in_specs=[SMEM_SPEC, HBM_SPEC, HBM_SPEC, HBM_SPEC, VMEM_SPEC] + [HBM_SPEC] * 9,
        out_specs=(HBM_SPEC,) * 9,
        scratch_shapes=[
            pltpu.SMEM((NODES,), jnp.int32),
            vmem16(SEG, WIDTH),
            vmem16(WIDTH, SEG),
            vmem16(WIDTH, SEG),
            vmem16(GROUP * SEG, HEAD_DIM),
            vmem16(GROUP * SEG, HEAD_DIM),
            vmem16(GROUP, DEEP, SEG),
            vmem16(SEG, WIDTH),
            vmem16(NODES, SEG, DEEP),
            vmem16(NODES, SEG, DEEP),
            vmem16(NODES, SEG, GROUP * SEG),
            vmem16(SEG, GROUP * SEG),
            vmem16(SIDE, SIDE, SEG, HEAD_DIM),
            vmem16(SIDE, SIDE, SEG, HEAD_DIM),
            vmem32(HEAD_DIM, GROUP * SEG),
            pltpu.SemaphoreType.DMA((2, NODES)),
            pltpu.SemaphoreType.DMA((NODES,)),
            pltpu.SemaphoreType.DMA((3,)),
        ],
        compiler_params=pltpu.CompilerParams(vmem_limit_bytes=VMEM_LIMIT),
        cost_estimate=pl.CostEstimate(flops=4 * 10**9, bytes_accessed=8 * 2**20, transcendentals=0),
        name="attend_grads",
    )(parent, queries, grad_t, out_t, inverse, *key_rows, *value_rows, weights)


def project_kernel(x_hbm, w_hbm, out_hbm, x_ref, w_ref, acc_ref, out_ref, x_sem, w_sem, out_sem):
    parts, _, width = x_ref.shape
    blocks = [slice(n * SEG, (n + 1) * SEG) for n in range(w_hbm.shape[0] // SEG)]

    def x_copy(t):
        return pltpu.make_async_copy(x_hbm.at[t], x_ref.at[t], x_sem.at[t])

    def w_copy(t, n):
        rows = pl.ds(n * SEG, SEG)
        return pltpu.make_async_copy(w_hbm.at[rows, pl.ds(t * width, width)], w_ref.at[t, rows], w_sem.at[t, n])

    for t in range(parts):
        x_copy(t).start()
        for n in range(len(blocks)):
            w_copy(t, n).start()
    for t in range(parts):
        x_copy(t).wait()
        for n in range(len(blocks)):
            w_copy(t, n).wait()
        x_t = x_ref[t].T
        for rows in blocks:
            part = matmul(w_ref[t, rows], x_t)
            if t == 0:
                acc_ref[rows] = part
            elif t < parts - 1:
                acc_ref[rows] += part
            else:
                out_ref[rows] = (acc_ref[rows] + part).astype(jnp.bfloat16)
    out_copy = pltpu.make_async_copy(out_ref, out_hbm, out_sem)
    out_copy.start()
    out_copy.wait()


def project(gathered, w_out):
    parts, rows, width = gathered.shape
    heads_wide = w_out.shape[0]
    return pl.pallas_call(
        project_kernel,
        out_shape=bf16(heads_wide, rows),
        in_specs=[HBM_SPEC] * 2,
        out_specs=HBM_SPEC,
        scratch_shapes=[
            vmem16(parts, rows, width),
            vmem16(parts, heads_wide, width),
            vmem32(heads_wide, rows),
            vmem16(heads_wide, rows),
            pltpu.SemaphoreType.DMA((parts,)),
            pltpu.SemaphoreType.DMA((parts, heads_wide // SEG)),
            pltpu.SemaphoreType.DMA,
        ],
        compiler_params=pltpu.CompilerParams(vmem_limit_bytes=VMEM_LIMIT),
        cost_estimate=pl.CostEstimate(flops=4 * 10**9, bytes_accessed=20 * 2**20, transcendentals=0),
        name="project",
    )(gathered, w_out)


def permute_line(blocks, along, sign):
    came = {step: lax.ppermute(blocks[step], "branch", along(sign * step)) for step in (1, 3, 2)}
    return [came[step] for step in (1, 2, 3)]


def gather_line(block, along):
    return [block] + permute_line([block] * SIDE, along, 1)


def add_up(parts):
    total = parts[0].astype(jnp.float32)
    for part in parts[1:]:
        total = total + part.astype(jnp.float32)
    return total.astype(jnp.bfloat16)


def per_device(queries, keys, values, grad_out, w_out, parent):
    gathered = lax.all_gather(grad_out, "tensor", axis=0)
    key_line, value_line = lax.optimization_barrier(
        (jnp.stack(gather_line(keys, along_x)), jnp.stack(gather_line(values, along_y)))
    )
    key_rows, value_rows = gather_line(key_line, along_y), gather_line(value_line, along_x)
    attn_out, out_t, inverse, weights = forward(parent, queries, key_rows, value_rows)
    grad_t = project(gathered, w_out)
    grad_queries, *lines = backward(parent, queries, grad_t, out_t, inverse, key_rows, value_rows, weights)
    key_parts = permute_line(lines[:SIDE], along_y, -1)
    value_parts = permute_line(lines[SIDE:], along_x, -1)
    value_sums = add_up([lines[SIDE]] + value_parts)
    key_sums = add_up([lines[0]] + key_parts)
    key_sums, value_sums = lax.optimization_barrier((key_sums, value_sums))
    value_parts = permute_line(value_sums, along_y, -1)
    key_parts = permute_line(key_sums, along_x, -1)
    return attn_out, grad_queries, add_up([key_sums[0]] + key_parts), add_up([value_sums[0]] + value_parts)


def solution(mesh):
    return jax.shard_map(
        per_device,
        mesh=mesh,
        in_specs=(
            P("branch", "tensor"),
            P("branch", "tensor"),
            P("branch", "tensor"),
            P("branch", "tensor"),
            P("tensor", None),
            P(),
        ),
        out_specs=(P("branch", "tensor"),) * 4,
        check_vma=False,
    )
```

```python
import functools
import math

import jax
import jax.numpy as jnp
from jax import lax
from jax.experimental import pallas as pl
from jax.experimental.pallas import tpu as pltpu
from jax.sharding import PartitionSpec as P

HEAD_DIM = 128
SEG = 256
NODES = 16
SIDE = 4
GROUP = 8
SCALE = 1.0 / math.sqrt(HEAD_DIM)
EXP2_SCALE = SCALE * math.log2(math.e)
NEG_FLOOR = -1e30
VMEM_LIMIT = 60 * 1024 * 1024
DEEP = 2 * HEAD_DIM
TILE = 16
SUM_LIMIT = 2.0**30
AHEAD = 3

NT = (((1,), (1,)), ((), ()))
NN = (((1,), (0,)), ((), ()))


def matmul(left, right, dims=NN):
    return lax.dot_general(left, right, dims, preferred_element_type=jnp.float32)


def list_visible(parent_ref, own, visible_ref):
    visible_ref[0] = own

    def climb(state):
        node, count = state
        above = parent_ref[node]
        visible_ref[count] = above
        return above, count + 1

    def has_parent(state):
        node, count = state
        return jnp.logical_and(parent_ref[node] >= 0, count < NODES)

    return lax.while_loop(has_parent, climb, (own, jnp.int32(1)))[1]


def ring(count, shift):
    return [(i, (i + shift) % count) for i in range(count)]


def along_x(shift):
    return [(y * SIDE + x, y * SIDE + (x + shift) % SIDE) for y in range(SIDE) for x in range(SIDE)]


def along_y(shift):
    return [(y * SIDE + x, ((y + shift) % SIDE) * SIDE + x) for y in range(SIDE) for x in range(SIDE)]


def offsets(own, node):
    behind_y = lax.rem(lax.div(own, SIDE) - lax.div(node, SIDE) + SIDE, SIDE)
    behind_x = lax.rem(lax.rem(own, SIDE) - lax.rem(node, SIDE) + SIDE, SIDE)
    return behind_y, behind_x


def start_keys(i, own, visible_ref, refs, buf, sem):
    behind_y, behind_x = offsets(own, visible_ref[i])
    for step in range(SIDE):

        @pl.when(behind_y == step)
        def _():
            pltpu.make_async_copy(refs[step].at[behind_x], buf.at[i, :, pl.ds(0, HEAD_DIM)], sem.at[i]).start()


def start_values(i, own, visible_ref, refs, buf, sem):
    behind_y, behind_x = offsets(own, visible_ref[i])
    for step in range(SIDE):

        @pl.when(behind_x == step)
        def _():
            pltpu.make_async_copy(refs[step].at[behind_y], buf.at[i, :, pl.ds(0, HEAD_DIM)], sem.at[i]).start()


def wait_block(i, ref, buf, sem):
    pltpu.make_async_copy(ref.at[0], buf.at[i, :, pl.ds(0, HEAD_DIM)], sem.at[i]).wait()


def repeat(first, last, do):
    def step(i, unused):
        do(i)
        return unused

    lax.fori_loop(first, last, step, 0)


def head(h):
    return slice(h * HEAD_DIM, (h + 1) * HEAD_DIM)


def head_rows(h):
    return slice(h * SEG, (h + 1) * SEG)


def unit_lanes(count):
    lane = lax.broadcasted_iota(jnp.int32, (SEG, HEAD_DIM), 1)
    return jnp.where(lane < count, 1.0, 0.0).astype(jnp.bfloat16)


def top_rows(rows):
    place = lax.broadcasted_iota(jnp.int32, (TILE, SEG), 0)
    tile = jnp.zeros((TILE, SEG), jnp.float32)
    for n, row in enumerate(rows):
        tile = jnp.where(place == n, row, tile)
    return tile.astype(jnp.bfloat16)


def rounded(values):
    return values.astype(jnp.bfloat16).astype(jnp.float32)


def forward_kernel(
    parent_ref, q_hbm, k0, k1, k2, k3, v0, v1, v2, v3, out_hbm, out_t_hbm, inverse_ref, weights_hbm,
    visible_ref, q_ref, q_deep_ref, out_ref, out_t_ref, key_buf, value_buf, values_t_ref, weights_buf,
    score_ref, acc_ref, max_ref, kv_sem, weights_sem, one_sem,
):
    key_refs, value_refs = (k0, k1, k2, k3), (v0, v1, v2, v3)
    own = lax.axis_index("branch")
    q_copy = pltpu.make_async_copy(q_hbm, q_ref, one_sem.at[0])
    q_copy.start()
    count = list_visible(parent_ref, own, visible_ref)
    repeat(0, count, lambda i: start_keys(i, own, visible_ref, key_refs, key_buf, kv_sem.at[0]))
    repeat(0, count, lambda i: start_values(i, own, visible_ref, value_refs, value_buf, kv_sem.at[1]))

    def fill(i):
        key_buf[i, :, HEAD_DIM:] = unit_lanes(1)

    repeat(0, count, fill)
    values_t_ref[HEAD_DIM:, :] = jnp.ones((TILE, SEG), jnp.bfloat16)
    q_deep_ref[:, HEAD_DIM:, :] = jnp.zeros((GROUP, HEAD_DIM, SEG), jnp.bfloat16)
    q_copy.wait()
    for h in range(GROUP):
        q_deep_ref[h, :HEAD_DIM, :] = q_ref[:, head(h)].T

    def weights_copy(i):
        return pltpu.make_async_copy(weights_buf.at[i], weights_hbm.at[i], weights_sem.at[i])

    def wait_kv(i):
        wait_block(i, k0, key_buf, kv_sem.at[0])
        wait_block(i, v0, value_buf, kv_sem.at[1])

    def set_shift(h, row):
        q_deep_ref[h, HEAD_DIM : HEAD_DIM + TILE, :] = top_rows([-row])

    def own_scores(h):
        key_pos = lax.broadcasted_iota(jnp.int32, (SEG, SEG), 0)
        row_pos = lax.broadcasted_iota(jnp.int32, (SEG, SEG), 1)
        return jnp.where(key_pos <= row_pos, matmul(key_buf[0], q_deep_ref[h]), NEG_FLOOR)

    def values_in(i):
        values_t_ref[:HEAD_DIM, :] = value_buf[i, :, :HEAD_DIM].T

    def block(i):
        values_in(i)
        for h in range(GROUP):
            weights = jnp.exp2(matmul(key_buf[i], q_deep_ref[h]) * EXP2_SCALE)
            weights_buf[i, :, head_rows(h)] = weights.astype(jnp.bfloat16)
        for h in range(GROUP):
            acc_ref[h] += matmul(values_t_ref[...], weights_buf[i, :, head_rows(h)])
        weights_copy(i).start()

    def own_block(scores_of):
        values_in(0)
        for h in range(GROUP):
            weights = jnp.exp2(scores_of(h) * EXP2_SCALE)
            weights_buf[0, :, head_rows(h)] = weights.astype(jnp.bfloat16)
        for h in range(GROUP):
            acc_ref[h] = matmul(values_t_ref[...], weights_buf[0, :, head_rows(h)])
        weights_copy(0).start()

    wait_kv(0)
    for h in range(GROUP):
        scores = own_scores(h)
        score_ref[h] = scores
        max_ref[h : h + 1, :] = rounded(jnp.max(scores, axis=0, keepdims=True))
    for h in range(GROUP):
        set_shift(h, max_ref[h : h + 1, :])
    own_block(lambda h: score_ref[h] - max_ref[h : h + 1, :])

    def first_visit(i):
        wait_kv(i)
        block(i)

    repeat(1, count, first_visit)
    sums = acc_ref[:, HEAD_DIM, :]
    too_large = jnp.max(jnp.where(sums < SUM_LIMIT, 0.0, 1.0)) > 0.0

    @pl.when(too_large)
    def _():
        repeat(0, count, lambda i: weights_copy(i).wait())
        for h in range(GROUP):
            set_shift(h, jnp.zeros((1, SEG), jnp.float32))

        def raise_max(i):
            for h in range(GROUP):
                block_max = jnp.max(matmul(key_buf[i], q_deep_ref[h]), axis=0, keepdims=True)
                max_ref[h : h + 1, :] = jnp.maximum(max_ref[h : h + 1, :], block_max)

        repeat(1, count, raise_max)
        for h in range(GROUP):
            set_shift(h, rounded(max_ref[h : h + 1, :]))
        own_block(own_scores)
        repeat(1, count, block)

    inverse = 1.0 / acc_ref[:, HEAD_DIM, :]
    inverse_ref[...] = inverse
    for h in range(GROUP):
        out = acc_ref[h, :HEAD_DIM, :] * inverse[h : h + 1, :]
        out_t_ref[head(h), :] = out.astype(jnp.bfloat16)
        out_ref[:, head(h)] = out.T.astype(jnp.bfloat16)
    copies = [
        pltpu.make_async_copy(out_ref, out_hbm, one_sem.at[1]),
        pltpu.make_async_copy(out_t_ref, out_t_hbm, one_sem.at[2]),
    ]
    for copy in copies:
        copy.start()
    repeat(0, count, lambda i: weights_copy(i).wait())
    for copy in copies:
        copy.wait()


SMEM_SPEC = pl.BlockSpec(memory_space=pltpu.SMEM)
VMEM_SPEC = pl.BlockSpec(memory_space=pltpu.VMEM)
HBM_SPEC = pl.BlockSpec(memory_space=pl.ANY)
WIDTH = GROUP * HEAD_DIM


def bf16(*shape):
    return jax.ShapeDtypeStruct(shape, jnp.bfloat16)


def vmem16(*shape):
    return pltpu.VMEM(shape, jnp.bfloat16)


def vmem32(*shape):
    return pltpu.VMEM(shape, jnp.float32)


def forward(parent, queries, key_rows, value_rows):
    return pl.pallas_call(
        forward_kernel,
        out_shape=(
            bf16(SEG, WIDTH),
            bf16(WIDTH, SEG),
            jax.ShapeDtypeStruct((GROUP, SEG), jnp.float32),
            bf16(NODES, SEG, GROUP * SEG),
        ),
        in_specs=[SMEM_SPEC] + [HBM_SPEC] * 9,
        out_specs=(HBM_SPEC, HBM_SPEC, VMEM_SPEC, HBM_SPEC),
        scratch_shapes=[
            pltpu.SMEM((NODES,), jnp.int32),
            vmem16(SEG, WIDTH),
            vmem16(GROUP, DEEP, SEG),
            vmem16(SEG, WIDTH),
            vmem16(WIDTH, SEG),
            vmem16(NODES, SEG, DEEP),
            vmem16(NODES, SEG, DEEP),
            vmem16(HEAD_DIM + TILE, SEG),
            vmem16(NODES, SEG, GROUP * SEG),
            vmem32(GROUP, SEG, SEG),
            vmem32(GROUP, HEAD_DIM + TILE, SEG),
            vmem32(GROUP, SEG),
            pltpu.SemaphoreType.DMA((2, NODES)),
            pltpu.SemaphoreType.DMA((NODES,)),
            pltpu.SemaphoreType.DMA((3,)),
        ],
        compiler_params=pltpu.CompilerParams(vmem_limit_bytes=VMEM_LIMIT),
        cost_estimate=pl.CostEstimate(flops=2 * 10**9, bytes_accessed=8 * 2**20, transcendentals=3 * 10**6),
        name="attend",
    )(parent, queries, *key_rows, *value_rows)


def grads_kernel(
    parent_ref, x_hbm, w_hbm, q_hbm, out_t_hbm, inverse_hbm, k0, k1, k2, k3, v0, v1, v2, v3, weights_hbm,
    dq_hbm, dk0, dk1, dk2, dk3, dv_hbm,
    visible_ref, x_ref, w_ref, out_t_ref, inverse_ref, q_tall_ref, key_buf, value_buf, weights_buf, acc_ref,
    grad_tall_ref, grad_deep_ref, dscore_ref, dk_ref, dv_ref, dq_acc, dq_ref,
    x_sem, w_sem, q_sem, kv_sem, weights_sem, small_sem,
):
    parts, _, width = x_ref.shape
    blocks = [slice(n * SEG, (n + 1) * SEG) for n in range(w_hbm.shape[0] // SEG)]

    def x_copy(t):
        return pltpu.make_async_copy(x_hbm.at[t], x_ref.at[t], x_sem.at[t])

    def w_copy(t, n):
        rows = pl.ds(n * SEG, SEG)
        return pltpu.make_async_copy(w_hbm.at[rows, pl.ds(t * width, width)], w_ref.at[t, rows], w_sem.at[t, n])

    def weights_copy(i):
        return pltpu.make_async_copy(weights_hbm.at[i], weights_buf.at[i], weights_sem.at[i])

    q_copies = [
        pltpu.make_async_copy(q_hbm.at[:, pl.ds(h * HEAD_DIM, HEAD_DIM)], q_tall_ref.at[pl.ds(h * SEG, SEG)], q_sem.at[h])
        for h in range(GROUP)
    ]
    small_copies = [
        pltpu.make_async_copy(out_t_hbm, out_t_ref, small_sem.at[0]),
        pltpu.make_async_copy(inverse_hbm, inverse_ref, small_sem.at[1]),
    ]
    def start_part(t):
        x_copy(t).start()
        for n in range(len(blocks)):
            w_copy(t, n).start()

    for t in range(AHEAD):
        start_part(t)
    own = lax.axis_index("branch")
    count = list_visible(parent_ref, own, visible_ref)

    def start(i):
        start_keys(i, own, visible_ref, (k0, k1, k2, k3), key_buf, kv_sem.at[0])
        start_values(i, own, visible_ref, (v0, v1, v2, v3), value_buf, kv_sem.at[1])
        weights_copy(i).start()

    def fill(i):
        value_buf[i, :, HEAD_DIM:] = unit_lanes(3)

    repeat(0, count, fill)
    dk_ref[...] = jnp.zeros_like(dk_ref)
    dv_ref[...] = jnp.zeros_like(dv_ref)
    dq_acc[...] = jnp.zeros_like(dq_acc)
    grad_deep_ref[:, HEAD_DIM:, :] = jnp.zeros((GROUP, HEAD_DIM, SEG), jnp.bfloat16)
    for t in range(parts):
        x_copy(t).wait()
        for n in range(len(blocks)):
            w_copy(t, n).wait()
        if t + AHEAD < parts:
            start_part(t + AHEAD)
        elif t + AHEAD == parts:
            for copy in small_copies + q_copies:
                copy.start()
            repeat(0, count, start)
        x_t = x_ref[t].T
        for rows in blocks:
            part = matmul(w_ref[t, rows], x_t)
            acc_ref[rows] = part if t == 0 else acc_ref[rows] + part
    for copy in small_copies + q_copies:
        copy.wait()
    for h in range(GROUP):
        grad_t = (rounded(acc_ref[head(h), :]) * inverse_ref[h : h + 1, :]).astype(jnp.bfloat16)
        grad_deep_ref[h, :HEAD_DIM, :] = grad_t
        grad_tall_ref[head_rows(h), :] = grad_t.T
        products = grad_t.astype(jnp.float32) * out_t_ref[head(h), :].astype(jnp.float32)
        delta = -jnp.sum(products, axis=0, keepdims=True)
        high = rounded(delta)
        middle = rounded(delta - high)
        grad_deep_ref[h, HEAD_DIM : HEAD_DIM + TILE, :] = top_rows([high, middle, delta - high - middle])

    def block(i):
        wait_block(i, k0, key_buf, kv_sem.at[0])
        wait_block(i, v0, value_buf, kv_sem.at[1])
        weights_copy(i).wait()
        keys_t = key_buf[i, :, :HEAD_DIM].T
        for h in range(GROUP):
            lowered = matmul(value_buf[i], grad_deep_ref[h])
            weights = weights_buf[i, :, head_rows(h)].astype(jnp.float32)
            dscore_ref[:, head_rows(h)] = (weights * lowered).astype(jnp.bfloat16)
        node = visible_ref[i]
        behind_y, behind_x = offsets(own, node)
        value_grad = matmul(weights_buf[i], grad_tall_ref[...])
        dv_ref[lax.rem(node, SIDE), behind_y] = value_grad.astype(jnp.bfloat16)
        key_grad = matmul(dscore_ref[...], q_tall_ref[...])
        dk_ref[behind_y, behind_x] = (key_grad * SCALE).astype(jnp.bfloat16)
        dq_acc[...] += matmul(keys_t, dscore_ref[...])

    repeat(0, count, block)
    stores = [
        pltpu.make_async_copy(dk_ref.at[n], target, kv_sem.at[0, n]) for n, target in enumerate((dk0, dk1, dk2, dk3))
    ] + [pltpu.make_async_copy(dv_ref, dv_hbm, kv_sem.at[1, 0])]
    for store in stores:
        store.start()
    for h in range(GROUP):
        dq_ref[:, head(h)] = (dq_acc[:, head_rows(h)] * SCALE).T.astype(jnp.bfloat16)
    dq_copy = pltpu.make_async_copy(dq_ref, dq_hbm, small_sem.at[0])
    dq_copy.start()
    for store in stores:
        store.wait()
    dq_copy.wait()


def grads(parent, gathered, w_out, queries, out_t, inverse, key_rows, value_rows, weights):
    parts, rows, width = gathered.shape
    return pl.pallas_call(
        grads_kernel,
        out_shape=(bf16(SEG, WIDTH),) + (bf16(SIDE, SEG, HEAD_DIM),) * 4 + (bf16(SIDE, SIDE, SEG, HEAD_DIM),),
        in_specs=[SMEM_SPEC] + [HBM_SPEC] * 14,
        out_specs=(HBM_SPEC,) * 6,
        scratch_shapes=[
            pltpu.SMEM((NODES,), jnp.int32),
            vmem16(parts, rows, width),
            vmem16(parts, w_out.shape[0], width),
            vmem16(WIDTH, SEG),
            vmem32(GROUP, SEG),
            vmem16(GROUP * SEG, HEAD_DIM),
            vmem16(NODES, SEG, DEEP),
            vmem16(NODES, SEG, DEEP),
            vmem16(NODES, SEG, GROUP * SEG),
            vmem32(WIDTH, SEG),
            vmem16(GROUP * SEG, HEAD_DIM),
            vmem16(GROUP, DEEP, SEG),
            vmem16(SEG, GROUP * SEG),
            vmem16(SIDE, SIDE, SEG, HEAD_DIM),
            vmem16(SIDE, SIDE, SEG, HEAD_DIM),
            vmem32(HEAD_DIM, GROUP * SEG),
            vmem16(SEG, WIDTH),
            pltpu.SemaphoreType.DMA((parts,)),
            pltpu.SemaphoreType.DMA((parts, w_out.shape[0] // SEG)),
            pltpu.SemaphoreType.DMA((GROUP,)),
            pltpu.SemaphoreType.DMA((2, NODES)),
            pltpu.SemaphoreType.DMA((NODES,)),
            pltpu.SemaphoreType.DMA((2,)),
        ],
        compiler_params=pltpu.CompilerParams(vmem_limit_bytes=VMEM_LIMIT),
        cost_estimate=pl.CostEstimate(flops=9 * 10**9, bytes_accessed=30 * 2**20, transcendentals=0),
        name="grads",
    )(parent, gathered, w_out, queries, out_t, inverse, *key_rows, *value_rows, weights)


def permute_line(blocks, along, sign):
    came = {step: lax.ppermute(blocks[step], "branch", along(sign * step)) for step in (1, 3, 2)}
    return [came[step] for step in (1, 2, 3)]


def gather_line(block, along):
    return [block] + permute_line([block] * SIDE, along, 1)


def add_up(parts):
    total = parts[0].astype(jnp.float32)
    for part in parts[1:]:
        total = total + part.astype(jnp.float32)
    return total.astype(jnp.bfloat16)


LINES_X = [[y * SIDE + x for x in range(SIDE)] for y in range(SIDE)]


def per_device(queries, keys, values, grad_out, w_out, parent):
    gathered = lax.all_gather(grad_out, "tensor", axis=0)
    key_line, value_line = lax.optimization_barrier(
        (jnp.stack(gather_line(keys, along_x)), jnp.stack(gather_line(values, along_y)))
    )
    key_rows, value_rows = gather_line(key_line, along_y), gather_line(value_line, along_x)
    attn_out, out_t, inverse, weights = forward(parent, queries, key_rows, value_rows)
    grad_queries, *key_lines, value_lines = grads(
        parent, gathered, w_out, queries, out_t, inverse, key_rows, value_rows, weights
    )
    key_sums = add_up([key_lines[0]] + permute_line(key_lines, along_y, -1))
    grad_keys = add_up([key_sums[0]] + permute_line(key_sums, along_x, -1))
    value_sums = add_up(lax.all_to_all(value_lines, "branch", 0, 0, axis_index_groups=LINES_X))
    grad_values = add_up([value_sums[0]] + permute_line(value_sums, along_y, -1))
    return attn_out, grad_queries, grad_keys, grad_values


def solution(mesh):
    return jax.shard_map(
        per_device,
        mesh=mesh,
        in_specs=(
            P("branch", "tensor"),
            P("branch", "tensor"),
            P("branch", "tensor"),
            P("branch", "tensor"),
            P("tensor", None),
            P(),
        ),
        out_specs=(P("branch", "tensor"),) * 4,
        check_vma=False,
    )
```

```python
import functools
import math

import jax
import jax.numpy as jnp
from jax import lax
from jax.experimental import pallas as pl
from jax.experimental.pallas import tpu as pltpu
from jax.sharding import PartitionSpec as P

HEAD_DIM = 128
SEG = 256
NODES = 16
SIDE = 4
GROUP = 8
SCALE = 1.0 / math.sqrt(HEAD_DIM)
EXP2_SCALE = SCALE * math.log2(math.e)
NEG_FLOOR = -1e30
VMEM_LIMIT = 60 * 1024 * 1024
DEEP = 2 * HEAD_DIM
TILE = 16
SUM_LIMIT = 2.0**30
AHEAD = 3

NT = (((1,), (1,)), ((), ()))
NN = (((1,), (0,)), ((), ()))


def matmul(left, right, dims=NN):
    return lax.dot_general(left, right, dims, preferred_element_type=jnp.float32)


def list_visible(parent_ref, own, visible_ref):
    visible_ref[0] = own

    def climb(state):
        node, count = state
        above = parent_ref[node]
        visible_ref[count] = above
        return above, count + 1

    def has_parent(state):
        node, count = state
        return jnp.logical_and(parent_ref[node] >= 0, count < NODES)

    return lax.while_loop(has_parent, climb, (own, jnp.int32(1)))[1]


def ring(count, shift):
    return [(i, (i + shift) % count) for i in range(count)]


def along_x(shift):
    return [(y * SIDE + x, y * SIDE + (x + shift) % SIDE) for y in range(SIDE) for x in range(SIDE)]


def along_y(shift):
    return [(y * SIDE + x, ((y + shift) % SIDE) * SIDE + x) for y in range(SIDE) for x in range(SIDE)]


def offsets(own, node):
    behind_y = lax.rem(lax.div(own, SIDE) - lax.div(node, SIDE) + SIDE, SIDE)
    behind_x = lax.rem(lax.rem(own, SIDE) - lax.rem(node, SIDE) + SIDE, SIDE)
    return behind_y, behind_x


def start_keys(i, own, visible_ref, refs, buf, sem):
    behind_y, behind_x = offsets(own, visible_ref[i])
    for step in range(SIDE):

        @pl.when(behind_y == step)
        def _():
            pltpu.make_async_copy(refs[step].at[behind_x], buf.at[i, :, pl.ds(0, HEAD_DIM)], sem.at[i]).start()


def start_values(i, own, visible_ref, refs, buf, sem):
    behind_y, behind_x = offsets(own, visible_ref[i])
    for step in range(SIDE):

        @pl.when(behind_x == step)
        def _():
            pltpu.make_async_copy(refs[step].at[behind_y], buf.at[i, :, pl.ds(0, HEAD_DIM)], sem.at[i]).start()


def wait_block(i, ref, buf, sem):
    pltpu.make_async_copy(ref.at[0], buf.at[i, :, pl.ds(0, HEAD_DIM)], sem.at[i]).wait()


def repeat(first, last, do):
    def step(i, unused):
        do(i)
        return unused

    lax.fori_loop(first, last, step, 0)


def head(h):
    return slice(h * HEAD_DIM, (h + 1) * HEAD_DIM)


def head_rows(h):
    return slice(h * SEG, (h + 1) * SEG)


def unit_lanes(count):
    lane = lax.broadcasted_iota(jnp.int32, (SEG, HEAD_DIM), 1)
    return jnp.where(lane < count, 1.0, 0.0).astype(jnp.bfloat16)


def top_rows(rows):
    place = lax.broadcasted_iota(jnp.int32, (TILE, SEG), 0)
    tile = jnp.zeros((TILE, SEG), jnp.float32)
    for n, row in enumerate(rows):
        tile = jnp.where(place == n, row, tile)
    return tile.astype(jnp.bfloat16)


def rounded(values):
    return values.astype(jnp.bfloat16).astype(jnp.float32)


def forward_kernel(
    parent_ref, q_hbm, k0, k1, k2, k3, v0, v1, v2, v3, out_hbm, out_t_hbm, inverse_ref, weights_hbm,
    visible_ref, q_ref, q_deep_ref, out_ref, out_t_ref, key_buf, value_buf, values_t_ref, weights_buf,
    score_ref, acc_ref, max_ref, kv_sem, weights_sem, q_sem, out_sem,
):
    key_refs, value_refs = (k0, k1, k2, k3), (v0, v1, v2, v3)
    own = lax.axis_index("branch")
    q_copies = [pltpu.make_async_copy(q_hbm.at[:, pl.ds(h * HEAD_DIM, HEAD_DIM)], q_ref.at[:, pl.ds(h * HEAD_DIM, HEAD_DIM)], q_sem.at[h]) for h in range(GROUP)]
    for copy in q_copies:
        copy.start()
    count = list_visible(parent_ref, own, visible_ref)
    repeat(0, count, lambda i: start_keys(i, own, visible_ref, key_refs, key_buf, kv_sem.at[0]))
    repeat(0, count, lambda i: start_values(i, own, visible_ref, value_refs, value_buf, kv_sem.at[1]))

    def fill(i):
        key_buf[i, :, HEAD_DIM:] = unit_lanes(1)

    repeat(0, count, fill)
    values_t_ref[HEAD_DIM:, :] = jnp.ones((TILE, SEG), jnp.bfloat16)
    q_deep_ref[:, HEAD_DIM:, :] = jnp.zeros((GROUP, HEAD_DIM, SEG), jnp.bfloat16)
    for h in range(GROUP):
        q_copies[h].wait()
        q_deep_ref[h, :HEAD_DIM, :] = q_ref[:, head(h)].T

    def weights_copy(i):
        return pltpu.make_async_copy(weights_buf.at[i], weights_hbm.at[i], weights_sem.at[i])

    def wait_kv(i):
        wait_block(i, k0, key_buf, kv_sem.at[0])
        wait_block(i, v0, value_buf, kv_sem.at[1])

    def set_shift(h, row):
        q_deep_ref[h, HEAD_DIM : HEAD_DIM + TILE, :] = top_rows([-row])

    def own_scores(h):
        key_pos = lax.broadcasted_iota(jnp.int32, (SEG, SEG), 0)
        row_pos = lax.broadcasted_iota(jnp.int32, (SEG, SEG), 1)
        return jnp.where(key_pos <= row_pos, matmul(key_buf[0], q_deep_ref[h]), NEG_FLOOR)

    def values_in(i):
        values_t_ref[:HEAD_DIM, :] = value_buf[i, :, :HEAD_DIM].T

    def block(i):
        values_in(i)
        for h in range(GROUP):
            weights = jnp.exp2(matmul(key_buf[i], q_deep_ref[h]) * EXP2_SCALE)
            weights_buf[i, :, head_rows(h)] = weights.astype(jnp.bfloat16)
        for h in range(GROUP):
            acc_ref[h] += matmul(values_t_ref[...], weights_buf[i, :, head_rows(h)])
        weights_copy(i).start()

    def own_block(scores_of):
        values_in(0)
        for h in range(GROUP):
            weights = jnp.exp2(scores_of(h) * EXP2_SCALE)
            weights_buf[0, :, head_rows(h)] = weights.astype(jnp.bfloat16)
        for h in range(GROUP):
            acc_ref[h] = matmul(values_t_ref[...], weights_buf[0, :, head_rows(h)])
        weights_copy(0).start()

    wait_kv(0)
    for h in range(GROUP):
        scores = own_scores(h)
        score_ref[h] = scores
        max_ref[h : h + 1, :] = rounded(jnp.max(scores, axis=0, keepdims=True))
    for h in range(GROUP):
        set_shift(h, max_ref[h : h + 1, :])
    own_block(lambda h: score_ref[h] - max_ref[h : h + 1, :])

    def first_visit(i):
        wait_kv(i)
        block(i)

    repeat(1, count, first_visit)
    sums = acc_ref[:, HEAD_DIM, :]
    too_large = jnp.max(jnp.where(sums < SUM_LIMIT, 0.0, 1.0)) > 0.0

    @pl.when(too_large)
    def _():
        repeat(0, count, lambda i: weights_copy(i).wait())
        for h in range(GROUP):
            set_shift(h, jnp.zeros((1, SEG), jnp.float32))

        def raise_max(i):
            for h in range(GROUP):
                block_max = jnp.max(matmul(key_buf[i], q_deep_ref[h]), axis=0, keepdims=True)
                max_ref[h : h + 1, :] = jnp.maximum(max_ref[h : h + 1, :], block_max)

        repeat(1, count, raise_max)
        for h in range(GROUP):
            set_shift(h, rounded(max_ref[h : h + 1, :]))
        own_block(own_scores)
        repeat(1, count, block)

    inverse = 1.0 / acc_ref[:, HEAD_DIM, :]
    inverse_ref[...] = inverse
    copies = []
    for h in range(GROUP):
        out = acc_ref[h, :HEAD_DIM, :] * inverse[h : h + 1, :]
        out_t_ref[head(h), :] = out.astype(jnp.bfloat16)
        out_ref[:, head(h)] = out.T.astype(jnp.bfloat16)
        copies.append(pltpu.make_async_copy(out_ref.at[:, pl.ds(h * HEAD_DIM, HEAD_DIM)], out_hbm.at[:, pl.ds(h * HEAD_DIM, HEAD_DIM)], out_sem.at[0, h]))
        copies.append(pltpu.make_async_copy(out_t_ref.at[pl.ds(h * HEAD_DIM, HEAD_DIM)], out_t_hbm.at[pl.ds(h * HEAD_DIM, HEAD_DIM)], out_sem.at[1, h]))
        for copy in copies[-2:]:
            copy.start()
    repeat(0, count, lambda i: weights_copy(i).wait())
    for copy in copies:
        copy.wait()


SMEM_SPEC = pl.BlockSpec(memory_space=pltpu.SMEM)
VMEM_SPEC = pl.BlockSpec(memory_space=pltpu.VMEM)
HBM_SPEC = pl.BlockSpec(memory_space=pl.ANY)
WIDTH = GROUP * HEAD_DIM


def bf16(*shape):
    return jax.ShapeDtypeStruct(shape, jnp.bfloat16)


def vmem16(*shape):
    return pltpu.VMEM(shape, jnp.bfloat16)


def vmem32(*shape):
    return pltpu.VMEM(shape, jnp.float32)


def forward(parent, queries, key_rows, value_rows):
    return pl.pallas_call(
        forward_kernel,
        out_shape=(
            bf16(SEG, WIDTH),
            bf16(WIDTH, SEG),
            jax.ShapeDtypeStruct((GROUP, SEG), jnp.float32),
            bf16(NODES, SEG, GROUP * SEG),
        ),
        in_specs=[SMEM_SPEC] + [HBM_SPEC] * 9,
        out_specs=(HBM_SPEC, HBM_SPEC, VMEM_SPEC, HBM_SPEC),
        scratch_shapes=[
            pltpu.SMEM((NODES,), jnp.int32),
            vmem16(SEG, WIDTH),
            vmem16(GROUP, DEEP, SEG),
            vmem16(SEG, WIDTH),
            vmem16(WIDTH, SEG),
            vmem16(NODES, SEG, DEEP),
            vmem16(NODES, SEG, DEEP),
            vmem16(HEAD_DIM + TILE, SEG),
            vmem16(NODES, SEG, GROUP * SEG),
            vmem32(GROUP, SEG, SEG),
            vmem32(GROUP, HEAD_DIM + TILE, SEG),
            vmem32(GROUP, SEG),
            pltpu.SemaphoreType.DMA((2, NODES)),
            pltpu.SemaphoreType.DMA((NODES,)),
            pltpu.SemaphoreType.DMA((GROUP,)),
            pltpu.SemaphoreType.DMA((2, GROUP)),
        ],
        compiler_params=pltpu.CompilerParams(vmem_limit_bytes=VMEM_LIMIT),
        cost_estimate=pl.CostEstimate(flops=2 * 10**9, bytes_accessed=8 * 2**20, transcendentals=3 * 10**6),
        name="attend",
    )(parent, queries, *key_rows, *value_rows)


def grads_kernel(
    parent_ref, x_hbm, w_hbm, q_hbm, out_t_hbm, inverse_hbm, k0, k1, k2, k3, v0, v1, v2, v3, weights_hbm,
    dq_hbm, dk0, dk1, dk2, dk3, dv_hbm,
    visible_ref, x_ref, w_ref, out_t_ref, inverse_ref, q_tall_ref, key_buf, value_buf, weights_buf, acc_ref,
    grad_tall_ref, grad_deep_ref, dscore_ref, dk_ref, dv_ref, dq_acc, dq_ref,
    x_sem, w_sem, q_sem, kv_sem, weights_sem, small_sem,
):
    parts, _, width = x_ref.shape
    blocks = [slice(n * SEG, (n + 1) * SEG) for n in range(w_hbm.shape[0] // SEG)]

    def x_copy(t):
        return pltpu.make_async_copy(x_hbm.at[t], x_ref.at[t], x_sem.at[t])

    def w_copy(t, n):
        rows = pl.ds(n * SEG, SEG)
        return pltpu.make_async_copy(w_hbm.at[rows, pl.ds(t * width, width)], w_ref.at[t, rows], w_sem.at[t, n])

    def weights_copy(i):
        return pltpu.make_async_copy(weights_hbm.at[i], weights_buf.at[i], weights_sem.at[i])

    q_copies = [
        pltpu.make_async_copy(q_hbm.at[:, pl.ds(h * HEAD_DIM, HEAD_DIM)], q_tall_ref.at[pl.ds(h * SEG, SEG)], q_sem.at[h])
        for h in range(GROUP)
    ]
    small_copies = [
        pltpu.make_async_copy(out_t_hbm, out_t_ref, small_sem.at[0]),
        pltpu.make_async_copy(inverse_hbm, inverse_ref, small_sem.at[1]),
    ]
    def start_part(t):
        x_copy(t).start()
        for n in range(len(blocks)):
            w_copy(t, n).start()

    for t in range(AHEAD):
        start_part(t)
    own = lax.axis_index("branch")
    count = list_visible(parent_ref, own, visible_ref)

    def start(i):
        start_keys(i, own, visible_ref, (k0, k1, k2, k3), key_buf, kv_sem.at[0])
        start_values(i, own, visible_ref, (v0, v1, v2, v3), value_buf, kv_sem.at[1])
        weights_copy(i).start()

    def fill(i):
        value_buf[i, :, HEAD_DIM:] = unit_lanes(3)

    repeat(0, count, fill)
    dk_ref[...] = jnp.zeros_like(dk_ref)
    dv_ref[...] = jnp.zeros_like(dv_ref)
    dq_acc[...] = jnp.zeros_like(dq_acc)
    grad_deep_ref[:, HEAD_DIM:, :] = jnp.zeros((GROUP, HEAD_DIM, SEG), jnp.bfloat16)
    for t in range(parts):
        x_copy(t).wait()
        for n in range(len(blocks)):
            w_copy(t, n).wait()
        if t + AHEAD < parts:
            start_part(t + AHEAD)
        elif t + AHEAD == parts:
            for copy in small_copies + q_copies:
                copy.start()
            repeat(0, count, start)
        x_t = x_ref[t].T
        for rows in blocks:
            part = matmul(w_ref[t, rows], x_t)
            acc_ref[rows] = part if t == 0 else acc_ref[rows] + part
    for copy in small_copies + q_copies:
        copy.wait()
    for h in range(GROUP):
        grad_t = (rounded(acc_ref[head(h), :]) * inverse_ref[h : h + 1, :]).astype(jnp.bfloat16)
        grad_deep_ref[h, :HEAD_DIM, :] = grad_t
        grad_tall_ref[head_rows(h), :] = grad_t.T
        products = grad_t.astype(jnp.float32) * out_t_ref[head(h), :].astype(jnp.float32)
        delta = -jnp.sum(products, axis=0, keepdims=True)
        high = rounded(delta)
        middle = rounded(delta - high)
        grad_deep_ref[h, HEAD_DIM : HEAD_DIM + TILE, :] = top_rows([high, middle, delta - high - middle])

    def block(i):
        wait_block(i, k0, key_buf, kv_sem.at[0])
        wait_block(i, v0, value_buf, kv_sem.at[1])
        weights_copy(i).wait()
        keys_t = key_buf[i, :, :HEAD_DIM].T
        for h in range(GROUP):
            lowered = matmul(value_buf[i], grad_deep_ref[h])
            weights = weights_buf[i, :, head_rows(h)].astype(jnp.float32)
            dscore_ref[:, head_rows(h)] = (weights * lowered).astype(jnp.bfloat16)
        node = visible_ref[i]
        behind_y, behind_x = offsets(own, node)
        value_grad = matmul(weights_buf[i], grad_tall_ref[...])
        dv_ref[lax.rem(node, SIDE), behind_y] = value_grad.astype(jnp.bfloat16)
        key_grad = matmul(dscore_ref[...], q_tall_ref[...])
        dk_ref[behind_y, behind_x] = (key_grad * SCALE).astype(jnp.bfloat16)
        dq_acc[...] += matmul(keys_t, dscore_ref[...])

    repeat(0, count, block)
    stores = [
        pltpu.make_async_copy(dk_ref.at[n], target, kv_sem.at[0, n]) for n, target in enumerate((dk0, dk1, dk2, dk3))
    ] + [pltpu.make_async_copy(dv_ref, dv_hbm, kv_sem.at[1, 0])]
    for store in stores:
        store.start()
    for h in range(GROUP):
        dq_ref[:, head(h)] = (dq_acc[:, head_rows(h)] * SCALE).T.astype(jnp.bfloat16)
    dq_copy = pltpu.make_async_copy(dq_ref, dq_hbm, small_sem.at[0])
    dq_copy.start()
    for store in stores:
        store.wait()
    dq_copy.wait()


def grads(parent, gathered, w_out, queries, out_t, inverse, key_rows, value_rows, weights):
    parts, rows, width = gathered.shape
    return pl.pallas_call(
        grads_kernel,
        out_shape=(bf16(SEG, WIDTH),) + (bf16(SIDE, SEG, HEAD_DIM),) * 4 + (bf16(SIDE, SIDE, SEG, HEAD_DIM),),
        in_specs=[SMEM_SPEC] + [HBM_SPEC] * 14,
        out_specs=(HBM_SPEC,) * 6,
        scratch_shapes=[
            pltpu.SMEM((NODES,), jnp.int32),
            vmem16(parts, rows, width),
            vmem16(parts, w_out.shape[0], width),
            vmem16(WIDTH, SEG),
            vmem32(GROUP, SEG),
            vmem16(GROUP * SEG, HEAD_DIM),
            vmem16(NODES, SEG, DEEP),
            vmem16(NODES, SEG, DEEP),
            vmem16(NODES, SEG, GROUP * SEG),
            vmem32(WIDTH, SEG),
            vmem16(GROUP * SEG, HEAD_DIM),
            vmem16(GROUP, DEEP, SEG),
            vmem16(SEG, GROUP * SEG),
            vmem16(SIDE, SIDE, SEG, HEAD_DIM),
            vmem16(SIDE, SIDE, SEG, HEAD_DIM),
            vmem32(HEAD_DIM, GROUP * SEG),
            vmem16(SEG, WIDTH),
            pltpu.SemaphoreType.DMA((parts,)),
            pltpu.SemaphoreType.DMA((parts, w_out.shape[0] // SEG)),
            pltpu.SemaphoreType.DMA((GROUP,)),
            pltpu.SemaphoreType.DMA((2, NODES)),
            pltpu.SemaphoreType.DMA((NODES,)),
            pltpu.SemaphoreType.DMA((2,)),
        ],
        compiler_params=pltpu.CompilerParams(vmem_limit_bytes=VMEM_LIMIT),
        cost_estimate=pl.CostEstimate(flops=9 * 10**9, bytes_accessed=30 * 2**20, transcendentals=0),
        name="grads",
    )(parent, gathered, w_out, queries, out_t, inverse, *key_rows, *value_rows, weights)


def permute_line(blocks, along, sign):
    came = {step: lax.ppermute(blocks[step], "branch", along(sign * step)) for step in (1, 3, 2)}
    return [came[step] for step in (1, 2, 3)]


def gather_line(block, along):
    return [block] + permute_line([block] * SIDE, along, 1)


def add_up(parts):
    total = parts[0].astype(jnp.float32)
    for part in parts[1:]:
        total = total + part.astype(jnp.float32)
    return total.astype(jnp.bfloat16)


LINES_X = [[y * SIDE + x for x in range(SIDE)] for y in range(SIDE)]


def per_device(queries, keys, values, grad_out, w_out, parent):
    gathered = lax.all_gather(grad_out, "tensor", axis=0)
    key_line, value_line = lax.optimization_barrier(
        (jnp.stack(gather_line(keys, along_x)), jnp.stack(gather_line(values, along_y)))
    )
    key_rows, value_rows = gather_line(key_line, along_y), gather_line(value_line, along_x)
    attn_out, out_t, inverse, weights = forward(parent, queries, key_rows, value_rows)
    grad_queries, *key_lines, value_lines = grads(
        parent, gathered, w_out, queries, out_t, inverse, key_rows, value_rows, weights
    )
    key_sums = add_up([key_lines[0]] + permute_line(key_lines, along_y, -1))
    grad_keys = add_up([key_sums[0]] + permute_line(key_sums, along_x, -1))
    value_sums = add_up(lax.all_to_all(value_lines, "branch", 0, 0, axis_index_groups=LINES_X))
    grad_values = add_up([value_sums[0]] + permute_line(value_sums, along_y, -1))
    return attn_out, grad_queries, grad_keys, grad_values


def solution(mesh):
    return jax.shard_map(
        per_device,
        mesh=mesh,
        in_specs=(
            P("branch", "tensor"),
            P("branch", "tensor"),
            P("branch", "tensor"),
            P("branch", "tensor"),
            P("tensor", None),
            P(),
        ),
        out_specs=(P("branch", "tensor"),) * 4,
        check_vma=False,
    )
```

```python
import functools
import math

import jax
import jax.numpy as jnp
from jax import lax
from jax.experimental import pallas as pl
from jax.experimental.pallas import tpu as pltpu
from jax.sharding import PartitionSpec as P

HEAD_DIM = 128
SEG = 256
NODES = 16
SIDE = 4
GROUP = 8
SCALE = 1.0 / math.sqrt(HEAD_DIM)
EXP2_SCALE = SCALE * math.log2(math.e)
NEG_FLOOR = -1e30
VMEM_LIMIT = 60 * 1024 * 1024
DEEP = 2 * HEAD_DIM
TILE = 16
SUM_LIMIT = 2.0**30
AHEAD = 3
RING = 5

NT = (((1,), (1,)), ((), ()))
NN = (((1,), (0,)), ((), ()))


def matmul(left, right, dims=NN):
    return lax.dot_general(left, right, dims, preferred_element_type=jnp.float32)


def list_visible(parent_ref, own, visible_ref):
    visible_ref[0] = own

    def climb(state):
        node, count = state
        above = parent_ref[node]
        visible_ref[count] = above
        return above, count + 1

    def has_parent(state):
        node, count = state
        return jnp.logical_and(parent_ref[node] >= 0, count < NODES)

    return lax.while_loop(has_parent, climb, (own, jnp.int32(1)))[1]


def ring(count, shift):
    return [(i, (i + shift) % count) for i in range(count)]


def along_x(shift):
    return [(y * SIDE + x, y * SIDE + (x + shift) % SIDE) for y in range(SIDE) for x in range(SIDE)]


def along_y(shift):
    return [(y * SIDE + x, ((y + shift) % SIDE) * SIDE + x) for y in range(SIDE) for x in range(SIDE)]


def offsets(own, node):
    behind_y = lax.rem(lax.div(own, SIDE) - lax.div(node, SIDE) + SIDE, SIDE)
    behind_x = lax.rem(lax.rem(own, SIDE) - lax.rem(node, SIDE) + SIDE, SIDE)
    return behind_y, behind_x


def start_keys(i, own, visible_ref, refs, buf, sem):
    behind_y, behind_x = offsets(own, visible_ref[i])
    for step in range(SIDE):

        @pl.when(behind_y == step)
        def _():
            pltpu.make_async_copy(refs[step].at[behind_x], buf.at[i, :, pl.ds(0, HEAD_DIM)], sem.at[i]).start()


def start_values(i, own, visible_ref, refs, buf, sem):
    behind_y, behind_x = offsets(own, visible_ref[i])
    for step in range(SIDE):

        @pl.when(behind_x == step)
        def _():
            pltpu.make_async_copy(refs[step].at[behind_y], buf.at[i, :, pl.ds(0, HEAD_DIM)], sem.at[i]).start()


def wait_block(i, ref, buf, sem):
    pltpu.make_async_copy(ref.at[0], buf.at[i, :, pl.ds(0, HEAD_DIM)], sem.at[i]).wait()


def repeat(first, last, do):
    def step(i, unused):
        do(i)
        return unused

    lax.fori_loop(first, last, step, 0)


def head(h):
    return slice(h * HEAD_DIM, (h + 1) * HEAD_DIM)


def head_rows(h):
    return slice(h * SEG, (h + 1) * SEG)


def unit_lanes(count):
    lane = lax.broadcasted_iota(jnp.int32, (SEG, HEAD_DIM), 1)
    return jnp.where(lane < count, 1.0, 0.0).astype(jnp.bfloat16)


def top_rows(rows):
    place = lax.broadcasted_iota(jnp.int32, (TILE, SEG), 0)
    tile = jnp.zeros((TILE, SEG), jnp.float32)
    for n, row in enumerate(rows):
        tile = jnp.where(place == n, row, tile)
    return tile.astype(jnp.bfloat16)


def rounded(values):
    return values.astype(jnp.bfloat16).astype(jnp.float32)


def forward_kernel(
    parent_ref, q_hbm, k0, k1, k2, k3, v0, v1, v2, v3, out_hbm, out_t_hbm, inverse_ref, weights_hbm,
    visible_ref, q_ref, q_deep_ref, out_ref, out_t_ref, key_buf, value_buf, values_t_ref, weights_buf,
    score_ref, acc_ref, max_ref, kv_sem, weights_sem, one_sem,
):
    key_refs, value_refs = (k0, k1, k2, k3), (v0, v1, v2, v3)
    own = lax.axis_index("branch")
    q_copy = pltpu.make_async_copy(q_hbm, q_ref, one_sem.at[0])
    q_copy.start()
    count = list_visible(parent_ref, own, visible_ref)
    repeat(0, count, lambda i: start_keys(i, own, visible_ref, key_refs, key_buf, kv_sem.at[0]))
    repeat(0, count, lambda i: start_values(i, own, visible_ref, value_refs, value_buf, kv_sem.at[1]))

    def fill(i):
        key_buf[i, :, HEAD_DIM:] = unit_lanes(1)

    repeat(0, count, fill)
    values_t_ref[HEAD_DIM:, :] = jnp.ones((TILE, SEG), jnp.bfloat16)
    q_deep_ref[:, HEAD_DIM:, :] = jnp.zeros((GROUP, HEAD_DIM, SEG), jnp.bfloat16)
    q_copy.wait()
    for h in range(GROUP):
        q_deep_ref[h, :HEAD_DIM, :] = q_ref[:, head(h)].T

    def weights_copy(i):
        return pltpu.make_async_copy(weights_buf.at[i], weights_hbm.at[i], weights_sem.at[i])

    def wait_kv(i):
        wait_block(i, k0, key_buf, kv_sem.at[0])
        wait_block(i, v0, value_buf, kv_sem.at[1])

    def set_shift(h, row):
        q_deep_ref[h, HEAD_DIM : HEAD_DIM + TILE, :] = top_rows([-row])

    def own_scores(h):
        key_pos = lax.broadcasted_iota(jnp.int32, (SEG, SEG), 0)
        row_pos = lax.broadcasted_iota(jnp.int32, (SEG, SEG), 1)
        return jnp.where(key_pos <= row_pos, matmul(key_buf[0], q_deep_ref[h]), NEG_FLOOR)

    def values_in(i):
        values_t_ref[:HEAD_DIM, :] = value_buf[i, :, :HEAD_DIM].T

    def block(i):
        values_in(i)
        for h in range(GROUP):
            weights = jnp.exp2(matmul(key_buf[i], q_deep_ref[h]) * EXP2_SCALE)
            weights_buf[i, :, head_rows(h)] = weights.astype(jnp.bfloat16)
        for h in range(GROUP):
            acc_ref[h] += matmul(values_t_ref[...], weights_buf[i, :, head_rows(h)])
        weights_copy(i).start()

    def own_block(scores_of):
        values_in(0)
        for h in range(GROUP):
            weights = jnp.exp2(scores_of(h) * EXP2_SCALE)
            weights_buf[0, :, head_rows(h)] = weights.astype(jnp.bfloat16)
        for h in range(GROUP):
            acc_ref[h] = matmul(values_t_ref[...], weights_buf[0, :, head_rows(h)])
        weights_copy(0).start()

    wait_kv(0)
    for h in range(GROUP):
        scores = own_scores(h)
        score_ref[h] = scores
        max_ref[h : h + 1, :] = rounded(jnp.max(scores, axis=0, keepdims=True))
    for h in range(GROUP):
        set_shift(h, max_ref[h : h + 1, :])
    own_block(lambda h: score_ref[h] - max_ref[h : h + 1, :])

    def first_visit(i):
        wait_kv(i)
        block(i)

    repeat(1, count, first_visit)
    sums = acc_ref[:, HEAD_DIM, :]
    too_large = jnp.max(jnp.where(sums < SUM_LIMIT, 0.0, 1.0)) > 0.0

    @pl.when(too_large)
    def _():
        repeat(0, count, lambda i: weights_copy(i).wait())
        for h in range(GROUP):
            set_shift(h, jnp.zeros((1, SEG), jnp.float32))

        def raise_max(i):
            for h in range(GROUP):
                block_max = jnp.max(matmul(key_buf[i], q_deep_ref[h]), axis=0, keepdims=True)
                max_ref[h : h + 1, :] = jnp.maximum(max_ref[h : h + 1, :], block_max)

        repeat(1, count, raise_max)
        for h in range(GROUP):
            set_shift(h, rounded(max_ref[h : h + 1, :]))
        own_block(own_scores)
        repeat(1, count, block)

    inverse = 1.0 / acc_ref[:, HEAD_DIM, :]
    inverse_ref[...] = inverse
    for h in range(GROUP):
        out = acc_ref[h, :HEAD_DIM, :] * inverse[h : h + 1, :]
        out_t_ref[head(h), :] = out.astype(jnp.bfloat16)
        out_ref[:, head(h)] = out.T.astype(jnp.bfloat16)
    copies = [
        pltpu.make_async_copy(out_ref, out_hbm, one_sem.at[1]),
        pltpu.make_async_copy(out_t_ref, out_t_hbm, one_sem.at[2]),
    ]
    for copy in copies:
        copy.start()
    repeat(0, count, lambda i: weights_copy(i).wait())
    for copy in copies:
        copy.wait()


SMEM_SPEC = pl.BlockSpec(memory_space=pltpu.SMEM)
VMEM_SPEC = pl.BlockSpec(memory_space=pltpu.VMEM)
HBM_SPEC = pl.BlockSpec(memory_space=pl.ANY)
WIDTH = GROUP * HEAD_DIM


def bf16(*shape):
    return jax.ShapeDtypeStruct(shape, jnp.bfloat16)


def vmem16(*shape):
    return pltpu.VMEM(shape, jnp.bfloat16)


def vmem32(*shape):
    return pltpu.VMEM(shape, jnp.float32)


def forward(parent, queries, key_rows, value_rows):
    return pl.pallas_call(
        forward_kernel,
        out_shape=(
            bf16(SEG, WIDTH),
            bf16(WIDTH, SEG),
            jax.ShapeDtypeStruct((GROUP, SEG), jnp.float32),
            bf16(NODES, SEG, GROUP * SEG),
        ),
        in_specs=[SMEM_SPEC] + [HBM_SPEC] * 9,
        out_specs=(HBM_SPEC, HBM_SPEC, VMEM_SPEC, HBM_SPEC),
        scratch_shapes=[
            pltpu.SMEM((NODES,), jnp.int32),
            vmem16(SEG, WIDTH),
            vmem16(GROUP, DEEP, SEG),
            vmem16(SEG, WIDTH),
            vmem16(WIDTH, SEG),
            vmem16(NODES, SEG, DEEP),
            vmem16(NODES, SEG, DEEP),
            vmem16(HEAD_DIM + TILE, SEG),
            vmem16(NODES, SEG, GROUP * SEG),
            vmem32(GROUP, SEG, SEG),
            vmem32(GROUP, HEAD_DIM + TILE, SEG),
            vmem32(GROUP, SEG),
            pltpu.SemaphoreType.DMA((2, NODES)),
            pltpu.SemaphoreType.DMA((NODES,)),
            pltpu.SemaphoreType.DMA((3,)),
        ],
        compiler_params=pltpu.CompilerParams(vmem_limit_bytes=VMEM_LIMIT),
        cost_estimate=pl.CostEstimate(flops=2 * 10**9, bytes_accessed=8 * 2**20, transcendentals=3 * 10**6),
        name="attend",
    )(parent, queries, *key_rows, *value_rows)


def grads_kernel(
    parent_ref, x00, x01, x10, x11, x20, x21, x30, x31, x40, x41,
    w_hbm, q_hbm, out_t_hbm, inverse_hbm, k0, k1, k2, k3, v0, v1, v2, v3, weights_hbm,
    dq_hbm, dk0, dk1, dk2, dk3, dv_hbm,
    visible_ref, x_ref, w_ref, out_t_ref, inverse_ref, q_tall_ref, key_buf, value_buf, weights_buf, acc_ref,
    grad_tall_ref, grad_deep_ref, dscore_ref, dk_ref, dv_ref, dq_acc, dq_ref,
    x_sem, w_sem, q_sem, kv_sem, weights_sem, small_sem,
):
    parts, _, width = x_ref.shape
    blocks = [slice(n * SEG, (n + 1) * SEG) for n in range(w_hbm.shape[0] // SEG)]

    place = lax.axis_index("tensor")
    halves = (pl.ds(0, SEG // 2), pl.ds(SEG // 2, SEG // 2))
    sources = [(0, 0, x00), (0, 1, x01), (3, 0, x10), (3, 1, x11), (1, 0, x20), (1, 1, x21)]
    sources += [(2, 0, (x30, x40)), (2, 1, (x31, x41))]

    def x_copies(t):
        blocks_in = sources[t][2]
        if not isinstance(blocks_in, tuple):
            return [pltpu.make_async_copy(blocks_in, x_ref.at[t], x_sem.at[t, 0])]
        return [
            pltpu.make_async_copy(block, x_ref.at[t, rows], x_sem.at[t, n])
            for n, (block, rows) in enumerate(zip(blocks_in, halves))
        ]

    def w_columns(t):
        far, other, _ = sources[t]
        chip = lax.rem(lax.div(place, 2) + far, SIDE)
        core = lax.rem(place + other, 2)
        return pl.ds(pl.multiple_of((chip * 2 + core) * width, width), width)

    def w_copy(t, n):
        rows = pl.ds(n * SEG, SEG)
        return pltpu.make_async_copy(w_hbm.at[rows, w_columns(t)], w_ref.at[t % RING, rows], w_sem.at[t, n])

    def weights_copy(i):
        return pltpu.make_async_copy(weights_hbm.at[i], weights_buf.at[i], weights_sem.at[i])

    q_copies = [
        pltpu.make_async_copy(q_hbm.at[:, pl.ds(h * HEAD_DIM, HEAD_DIM)], q_tall_ref.at[pl.ds(h * SEG, SEG)], q_sem.at[h])
        for h in range(GROUP)
    ]
    def start_part(t):
        for copy in x_copies(t):
            copy.start()
        for n in range(len(blocks)):
            w_copy(t, n).start()

    small_copies = [
        pltpu.make_async_copy(out_t_hbm, out_t_ref, small_sem.at[0]),
        pltpu.make_async_copy(inverse_hbm, inverse_ref, small_sem.at[1]),
    ]
    for t in range(AHEAD):
        start_part(t)
    own = lax.axis_index("branch")
    count = list_visible(parent_ref, own, visible_ref)

    def start(i):
        start_keys(i, own, visible_ref, (k0, k1, k2, k3), key_buf, kv_sem.at[0])
        start_values(i, own, visible_ref, (v0, v1, v2, v3), value_buf, kv_sem.at[1])
        weights_copy(i).start()

    def fill(i):
        value_buf[i, :, HEAD_DIM:] = unit_lanes(3)

    repeat(0, count, fill)
    dk_ref[...] = jnp.zeros_like(dk_ref)
    dv_ref[...] = jnp.zeros_like(dv_ref)
    dq_acc[...] = jnp.zeros_like(dq_acc)
    grad_deep_ref[:, HEAD_DIM:, :] = jnp.zeros((GROUP, HEAD_DIM, SEG), jnp.bfloat16)
    for t in range(parts):
        for copy in x_copies(t):
            copy.wait()
        for n in range(len(blocks)):
            w_copy(t, n).wait()
        if t + AHEAD < parts:
            start_part(t + AHEAD)
        elif t + AHEAD == parts:
            for copy in small_copies + q_copies:
                copy.start()
            repeat(0, count, start)
        x_t = x_ref[t].T
        for rows in blocks:
            part = matmul(w_ref[t % RING, rows], x_t)
            acc_ref[rows] = part if t == 0 else acc_ref[rows] + part
    for copy in small_copies + q_copies:
        copy.wait()
    for h in range(GROUP):
        grad_t = (rounded(acc_ref[head(h), :]) * inverse_ref[h : h + 1, :]).astype(jnp.bfloat16)
        grad_deep_ref[h, :HEAD_DIM, :] = grad_t
        grad_tall_ref[head_rows(h), :] = grad_t.T
        products = grad_t.astype(jnp.float32) * out_t_ref[head(h), :].astype(jnp.float32)
        delta = -jnp.sum(products, axis=0, keepdims=True)
        high = rounded(delta)
        middle = rounded(delta - high)
        grad_deep_ref[h, HEAD_DIM : HEAD_DIM + TILE, :] = top_rows([high, middle, delta - high - middle])

    def block(i):
        wait_block(i, k0, key_buf, kv_sem.at[0])
        wait_block(i, v0, value_buf, kv_sem.at[1])
        weights_copy(i).wait()
        keys_t = key_buf[i, :, :HEAD_DIM].T
        for h in range(GROUP):
            lowered = matmul(value_buf[i], grad_deep_ref[h])
            weights = weights_buf[i, :, head_rows(h)].astype(jnp.float32)
            dscore_ref[:, head_rows(h)] = (weights * lowered).astype(jnp.bfloat16)
        node = visible_ref[i]
        behind_y, behind_x = offsets(own, node)
        value_grad = matmul(weights_buf[i], grad_tall_ref[...])
        dv_ref[lax.rem(node, SIDE), behind_y] = value_grad.astype(jnp.bfloat16)
        key_grad = matmul(dscore_ref[...], q_tall_ref[...])
        dk_ref[behind_y, behind_x] = (key_grad * SCALE).astype(jnp.bfloat16)
        dq_acc[...] += matmul(keys_t, dscore_ref[...])

    repeat(0, count, block)
    stores = [
        pltpu.make_async_copy(dk_ref.at[n], target, kv_sem.at[0, n]) for n, target in enumerate((dk0, dk1, dk2, dk3))
    ] + [pltpu.make_async_copy(dv_ref, dv_hbm, kv_sem.at[1, 0])]
    for store in stores:
        store.start()
    for h in range(GROUP):
        dq_ref[:, head(h)] = (dq_acc[:, head_rows(h)] * SCALE).T.astype(jnp.bfloat16)
    dq_copy = pltpu.make_async_copy(dq_ref, dq_hbm, small_sem.at[0])
    dq_copy.start()
    for store in stores:
        store.wait()
    dq_copy.wait()


def grads(parent, blocks, w_out, queries, out_t, inverse, key_rows, value_rows, weights):
    rows, width = blocks[0].shape
    parts = w_out.shape[1] // width
    return pl.pallas_call(
        grads_kernel,
        out_shape=(bf16(SEG, WIDTH),) + (bf16(SIDE, SEG, HEAD_DIM),) * 4 + (bf16(SIDE, SIDE, SEG, HEAD_DIM),),
        in_specs=[SMEM_SPEC] + [HBM_SPEC] * 23,
        out_specs=(HBM_SPEC,) * 6,
        scratch_shapes=[
            pltpu.SMEM((NODES,), jnp.int32),
            vmem16(parts, rows, width),
            vmem16(RING, w_out.shape[0], width),
            vmem16(WIDTH, SEG),
            vmem32(GROUP, SEG),
            vmem16(GROUP * SEG, HEAD_DIM),
            vmem16(NODES, SEG, DEEP),
            vmem16(NODES, SEG, DEEP),
            vmem16(NODES, SEG, GROUP * SEG),
            vmem32(WIDTH, SEG),
            vmem16(GROUP * SEG, HEAD_DIM),
            vmem16(GROUP, DEEP, SEG),
            vmem16(SEG, GROUP * SEG),
            vmem16(SIDE, SIDE, SEG, HEAD_DIM),
            vmem16(SIDE, SIDE, SEG, HEAD_DIM),
            vmem32(HEAD_DIM, GROUP * SEG),
            vmem16(SEG, WIDTH),
            pltpu.SemaphoreType.DMA((parts, 2)),
            pltpu.SemaphoreType.DMA((parts, w_out.shape[0] // SEG)),
            pltpu.SemaphoreType.DMA((GROUP,)),
            pltpu.SemaphoreType.DMA((2, NODES)),
            pltpu.SemaphoreType.DMA((NODES,)),
            pltpu.SemaphoreType.DMA((2,)),
        ],
        compiler_params=pltpu.CompilerParams(vmem_limit_bytes=VMEM_LIMIT),
        cost_estimate=pl.CostEstimate(flops=9 * 10**9, bytes_accessed=30 * 2**20, transcendentals=0),
        name="grads",
    )(parent, *blocks, w_out, queries, out_t, inverse, *key_rows, *value_rows, weights)


def permute_line(blocks, along, sign, order=(1, 3, 2)):
    came = {step: lax.ppermute(blocks[step], "branch", along(sign * step)) for step in order}
    return [came[step] for step in (1, 2, 3)]


def gather_line(block, along):
    return [block] + permute_line([block] * SIDE, along, 1)


def add_up(parts):
    total = parts[0].astype(jnp.float32)
    for part in parts[1:]:
        total = total + part.astype(jnp.float32)
    return total.astype(jnp.bfloat16)


LINES_X = [[y * SIDE + x for x in range(SIDE)] for y in range(SIDE)]


def along_z(shift):
    return [(z * 2 + core, (z + shift) % SIDE * 2 + core) for z in range(SIDE) for core in range(2)]


OTHER_CORE = [(n, n ^ 1) for n in range(2 * SIDE)]


def other_core(block):
    return lax.ppermute(block, "tensor", OTHER_CORE)


def per_device(queries, keys, values, grad_out, w_out, parent):
    middle = grad_out.shape[0] // 2
    up, down = lax.ppermute(grad_out, "tensor", along_z(1)), lax.ppermute(grad_out, "tensor", along_z(-1))
    key_line, value_line, up, down = lax.optimization_barrier(
        (jnp.stack(gather_line(keys, along_x)), jnp.stack(gather_line(values, along_y)), up, down)
    )
    far = (
        lax.ppermute(up[:middle], "tensor", along_z(1)),
        lax.ppermute(down[middle:], "tensor", along_z(-1)),
    )
    key_rows, value_rows, far = lax.optimization_barrier(
        (gather_line(key_line, along_y), gather_line(value_line, along_x), far)
    )
    blocks = [piece for block in (grad_out, up, down) + far for piece in (block, other_core(block))]
    attn_out, out_t, inverse, weights = forward(parent, queries, key_rows, value_rows)
    grad_queries, *key_lines, value_lines = grads(
        parent, blocks, w_out, queries, out_t, inverse, key_rows, value_rows, weights
    )
    key_sums = add_up([key_lines[0]] + permute_line(key_lines, along_y, -1))
    grad_keys = add_up([key_sums[0]] + permute_line(key_sums, along_x, -1))
    value_sums = add_up(lax.all_to_all(value_lines, "branch", 0, 0, axis_index_groups=LINES_X))
    grad_values = add_up([value_sums[0]] + permute_line(value_sums, along_y, -1))
    return attn_out, grad_queries, grad_keys, grad_values


def solution(mesh):
    return jax.shard_map(
        per_device,
        mesh=mesh,
        in_specs=(
            P("branch", "tensor"),
            P("branch", "tensor"),
            P("branch", "tensor"),
            P("branch", "tensor"),
            P("tensor", None),
            P(),
        ),
        out_specs=(P("branch", "tensor"),) * 4,
        check_vma=False,
    )
```
